256 devices in a mesh: gy: 16 (over x_lo, y, core), gz: 16 (over z, x_hi).
Axes of the slice: x: 4 (x_hi: 2, x_lo: 2; x = x_hi * 2 + x_lo), y: 4, z: 8, core: 2. Of those that a mesh axis runs over, the one named last changes fastest.
Arguments:
- phase: int32 [256, 256, 128], P('gy', 'gz'), may hold values from 0 to 1, as said below
- density: float32 [256, 256, 128], P('gy', 'gz'), may hold values from 0.8 to 1.2
- velocity: float32 [3, 256, 256, 128], P(None, 'gy', 'gz'), may hold values from -0.18 to 0.18
Outputs:
- density_red: float32 [256, 256, 128], P('gy', 'gz')
- density_blue: float32 [256, 256, 128], P('gy', 'gz')
- momentum: float32 [3, 256, 256, 128], P(None, 'gy', 'gz')
The draws below stay inside these ranges and needn't reach their ends.
Inputs may be any that keep to these rules, and one draw needn't show every extreme that they name: `phase`: 1 marks the liquid films of a periodic Weaire-Phelan foam (Voronoi cells of a jittered A15 lattice with cubic period 32); both labels occur.
All inputs are finite; a program needn't handle non-finite values.
Results may differ from the reference program's by a relative error of at most 0.00011.
Values sent between devices are 32-bit elements; how exact they have to be, the bound alone decides.
No kernel may reach another device: no remote copies, remote signals or barrier semaphores. Data moves between devices by JAX's collectives and lax.ppermute only.
A program may use at most 128 MiB of HBM per device.

```python
import math
import jax
import jax.numpy as jnp
from jax import lax

NX = 128
STEPS = 2
NY = 256
NZ = 256
PER = 32


def periodic_gap(coord, centre):
    offset = jnp.mod(coord - centre, PER)
    return jnp.minimum(offset, PER - offset)


def draw_phase(key, part):
    key = jax.random.fold_in(key, 11)
    shift_key, jitter_key = jax.random.split(key)
    shifts = jax.random.randint(shift_key, (3,), 0, PER)
    jitter = jax.random.randint(jitter_key, (8, 3), -1, 2)
    quarter = PER // 4
    sites = [[0, 0, 0], [2, 2, 2], [1, 2, 0], [3, 2, 0], [0, 1, 2], [0, 3, 2], [2, 0, 1], [2, 0, 3]]
    coord_y = jnp.arange(NY, dtype=jnp.int32)[:, None, None]
    coord_z = jnp.arange(NZ, dtype=jnp.int32)[None, :, None]
    coord_x = jnp.arange(NX, dtype=jnp.int32)[None, None, :]
    big = jnp.int32(3 * PER * PER)
    first = jnp.full((NY, NZ, NX), big, jnp.int32)
    second = jnp.full((NY, NZ, NX), big, jnp.int32)
    for number in range(8):
        site_x = sites[number][0] * quarter + shifts[0] + jitter[number, 0]
        site_y = sites[number][1] * quarter + shifts[1] + jitter[number, 1]
        site_z = sites[number][2] * quarter + shifts[2] + jitter[number, 2]
        gap_x = periodic_gap(coord_x, site_x)
        gap_y = periodic_gap(coord_y, site_y)
        gap_z = periodic_gap(coord_z, site_z)
        dist = gap_x * gap_x + gap_y * gap_y + gap_z * gap_z
        second = jnp.minimum(second, jnp.maximum(first, dist))
        first = jnp.minimum(first, dist)
    return (second - first < PER * PER // 10).astype(jnp.int32)


def steps_of(own_key, shape, cuts, low, top_value):
    factor_of = 1.0
    for axis_at, blocks in cuts:
        draws = jax.random.uniform(jax.random.fold_in(jax.random.fold_in(own_key, 6), axis_at), (blocks,), jnp.float32, low / len(cuts), top_value / len(cuts))
        factor_of = factor_of * jnp.repeat(jnp.exp(draws), shape[axis_at] // blocks).reshape((-1,) + (1,) * (len(shape) - 1 - axis_at))
    return factor_of


def noise(rng, shape, scale, most, pieces=(), kind=jnp.bfloat16):
    array = scale * jax.random.normal(rng, shape, jnp.float32)
    if pieces:
        array = array * steps_of(rng, shape, pieces, -0.22, 0.18)
    return jnp.clip(array, -most, most).astype(kind)


def setup_inputs(seed: int = 0) -> dict:
    key_of = jax.random.split(jax.random.key(seed), 4)
    phase = draw_phase(jax.random.fold_in(key_of[3], 71), 0)
    density = jnp.clip(0.8 + 0.40000004 * jax.random.uniform(key_of[1], (NY, NZ, NX), jnp.float32) ** steps_of(key_of[1], (NY, NZ, NX), ((0, 16), (1, 16)), -0.2, 0.2), 0.8, 1.2)
    velocity = noise(key_of[2], (3, NY, NZ, NX), 0.06, 0.18, ((1, 16), (2, 16)), jnp.float32)
    return dict(phase=phase, density=density, velocity=velocity)


VELOCITIES = [[0, 0, 0], [1, 0, 0], [-1, 0, 0], [0, 1, 0], [0, -1, 0], [0, 0, 1], [0, 0, -1], [1, 1, 0], [-1, -1, 0], [1, -1, 0], [-1, 1, 0], [1, 0, 1], [-1, 0, -1], [1, 0, -1], [-1, 0, 1], [0, 1, 1], [0, -1, -1], [0, 1, -1], [0, -1, 1]]
LATTICE_WEIGHTS = [1.0 / 3.0] + [1.0 / 18.0] * 6 + [1.0 / 36.0] * 12
BIASES = [-1.0 / 3.0] + [1.0 / 18.0] * 6 + [1.0 / 36.0] * 12
relax_time = 0.8
surface_amp = 0.05
recolouring_strength = 0.7
grad_floor = 0.05

def equilibrium(dens_in, vel_x, vel_y, vel_z):
    speed_sq = vel_x * vel_x + vel_y * vel_y + vel_z * vel_z
    result = []
    for site_index in range(19):
        c_x, c_y, c_z = [float(v) for v in VELOCITIES[site_index]]
        along_direction = c_x * vel_x + c_y * vel_y + c_z * vel_z
        result.append(LATTICE_WEIGHTS[site_index] * dens_in * (1.0 + 3.0 * along_direction + 4.5 * along_direction * along_direction - 1.5 * speed_sq))
    return jnp.stack(result)

def moments(total_pop):
    mom_x = total_pop[1] - total_pop[2] + total_pop[7] - total_pop[8] + total_pop[9] - total_pop[10] + total_pop[11] - total_pop[12] + total_pop[13] - total_pop[14]
    mom_y = total_pop[3] - total_pop[4] + total_pop[7] - total_pop[8] - total_pop[9] + total_pop[10] + total_pop[15] - total_pop[16] + total_pop[17] - total_pop[18]
    mom_z = total_pop[5] - total_pop[6] + total_pop[11] - total_pop[12] - total_pop[13] + total_pop[14] + total_pop[15] - total_pop[16] - total_pop[17] + total_pop[18]
    return (mom_x, mom_y, mom_z)

def densities(red_pop, blue_pop):
    rho_red = lax.optimization_barrier(jnp.sum(red_pop, axis=0))
    rho_blue = lax.optimization_barrier(jnp.sum(blue_pop, axis=0))
    dens_all = rho_red + rho_blue
    colour = (rho_red - rho_blue) / dens_all
    return (rho_red, rho_blue, dens_all, colour)

def collide(red_pop, blue_pop, rho_red, rho_blue, dens_all, nearby):
    grad_x = jnp.zeros_like(dens_all)
    grad_y = jnp.zeros_like(dens_all)
    grad_z = jnp.zeros_like(dens_all)
    for site_index in range(1, 19):
        c_x, c_y, c_z = [float(v) for v in VELOCITIES[site_index]]
        scaled = 3.0 * LATTICE_WEIGHTS[site_index] * nearby[site_index]
        grad_x = grad_x + c_x * scaled
        grad_y = grad_y + c_y * scaled
        grad_z = grad_z + c_z * scaled
    gmag = jnp.sqrt(grad_x * grad_x + grad_y * grad_y + grad_z * grad_z)
    gradient_divisor = jnp.maximum(gmag, grad_floor)
    total_pop = red_pop + blue_pop
    mom_x, mom_y, mom_z = moments(total_pop)
    feq = equilibrium(dens_all, mom_x / dens_all, mom_y / dens_all, mom_z / dens_all)
    share = rho_red / dens_all
    mixing_fraction = rho_red * rho_blue / dens_all
    red_out = []
    blue_out = []
    for site_index in range(19):
        c_x, c_y, c_z = [float(v) for v in VELOCITIES[site_index]]
        along_direction = c_x * grad_x + c_y * grad_y + c_z * grad_z
        post = total_pop[site_index] - (total_pop[site_index] - feq[site_index]) / relax_time + 0.5 * surface_amp * (LATTICE_WEIGHTS[site_index] * along_direction * along_direction / gradient_divisor - BIASES[site_index] * gmag)
        red_updated = share * post
        if site_index > 0:
            domain_length = math.sqrt(c_x * c_x + c_y * c_y + c_z * c_z)
            red_updated = red_updated + recolouring_strength * mixing_fraction * LATTICE_WEIGHTS[site_index] * along_direction / (domain_length * gradient_divisor)
        red_out.append(red_updated)
        blue_out.append(post - red_updated)
    return (jnp.stack(red_out), jnp.stack(blue_out))

def reference(phase, density, velocity):
    label = phase.astype(jnp.float32)
    red_pop = equilibrium(label * density, velocity[0], velocity[1], velocity[2])
    blue_pop = equilibrium((1.0 - label) * density, velocity[0], velocity[1], velocity[2])
    for step in range(STEPS):
        rho_red, rho_blue, dens_all, colour = densities(red_pop, blue_pop)
        nearby = []
        for site_index in range(19):
            c_x, c_y, c_z = [int(v) for v in VELOCITIES[site_index]]
            nearby.append(jnp.roll(colour, (-c_y, -c_z, -c_x), (0, 1, 2)))
        red_post, blue_post = collide(red_pop, blue_pop, rho_red, rho_blue, dens_all, nearby)
        red_list = []
        blue_list = []
        for site_index in range(19):
            c_x, c_y, c_z = [int(v) for v in VELOCITIES[site_index]]
            red_list.append(jnp.roll(red_post[site_index], (c_y, c_z, c_x), (0, 1, 2)))
            blue_list.append(jnp.roll(blue_post[site_index], (c_y, c_z, c_x), (0, 1, 2)))
        red_pop = jnp.stack(red_list)
        blue_pop = jnp.stack(blue_list)
    density_red = lax.optimization_barrier(jnp.sum(red_pop, axis=0))
    density_blue = lax.optimization_barrier(jnp.sum(blue_pop, axis=0))
    mom_x, mom_y, mom_z = moments(red_pop + blue_pop)
    return (density_red, density_blue, jnp.stack([mom_x, mom_y, mom_z]))
```

```python
import math

import jax
import jax.numpy as jnp
from jax import lax
from jax.experimental import pallas as pl
from jax.experimental.pallas import tpu as pltpu
from jax.sharding import PartitionSpec as P

VELOCITIES = [
    [0, 0, 0],
    [1, 0, 0],
    [-1, 0, 0],
    [0, 1, 0],
    [0, -1, 0],
    [0, 0, 1],
    [0, 0, -1],
    [1, 1, 0],
    [-1, -1, 0],
    [1, -1, 0],
    [-1, 1, 0],
    [1, 0, 1],
    [-1, 0, -1],
    [1, 0, -1],
    [-1, 0, 1],
    [0, 1, 1],
    [0, -1, -1],
    [0, 1, -1],
    [0, -1, 1],
]
INDEX = {tuple(v): i for i, v in enumerate(VELOCITIES)}
relax_time = 0.8
surface_amp = 0.05
recolouring_strength = 0.7
grad_floor = 0.05

WIDE = 4
VMEM = pltpu.CompilerParams(vmem_limit_bytes=48 * 1024 * 1024)


def rolled(value, shift):
    return pltpu.roll(value, shift % 128, 1) if shift else value


def fill_z(msg, low, phase, density, velocity):
    thin, wide = (0, 0) if low else (16 - 3, 16 - 4)
    msg[:, 0:3, :] = density[:, thin : thin + 3, :]
    for axis in range(3):
        msg[:, 3 + 3 * axis : 6 + 3 * axis, :] = velocity[axis, :, thin : thin + 3, :]
    msg[:, 12:16, :] = phase[:, wide : wide + 4, :].astype(jnp.float32)


def pack_z(phase, density, velocity, msg_ev, msg_od):
    odd = lax.rem(lax.axis_index("gz"), 2) == 1

    @pl.when(odd)
    def _():
        fill_z(msg_ev, True, phase, density, velocity)
        fill_z(msg_od, False, phase, density, velocity)

    @pl.when(jnp.logical_not(odd))
    def _():
        fill_z(msg_ev, False, phase, density, velocity)
        fill_z(msg_od, True, phase, density, velocity)


def put_z_halo(ref, row, at, msg, src, high):
    if at == 4:
        start = 20 if high else 0
        ref[row, start : start + 4, :] = msg[src, 12:16, :]
    else:
        start = 20 if high else 1
        ref[row, start : start + 3, :] = msg[src, 3 * at : 3 * at + 3, :]


def own_plane(at, y, phase, density, velocity):
    if at == 0:
        return density[y]
    if at == 4:
        return phase[y].astype(jnp.float32)
    return velocity[at - 1, y]


def fill_y(msg, low, odd_z, phase, density, velocity, from_ev, from_od):
    for at in range(5):
        count = 4 if at == 4 else 3
        for k in range(count):
            y = k if low else 16 - count + k
            row = 3 * at + k
            if at != 4:
                msg[row] = jnp.zeros((24, 128), jnp.float32)
            msg[row, 4:20, :] = own_plane(at, y, phase, density, velocity)

            @pl.when(odd_z)
            def _():
                put_z_halo(msg, row, at, from_ev, y, False)
                put_z_halo(msg, row, at, from_od, y, True)

            @pl.when(jnp.logical_not(odd_z))
            def _():
                put_z_halo(msg, row, at, from_od, y, False)
                put_z_halo(msg, row, at, from_ev, y, True)


def pack_y(phase, density, velocity, from_ev, from_od, msg_ev, msg_od):
    odd_z = lax.rem(lax.axis_index("gz"), 2) == 1
    odd_y = lax.rem(lax.axis_index("gy"), 2) == 1
    args = (odd_z, phase, density, velocity, from_ev, from_od)

    @pl.when(odd_y)
    def _():
        fill_y(msg_ev, True, *args)
        fill_y(msg_od, False, *args)

    @pl.when(jnp.logical_not(odd_y))
    def _():
        fill_y(msg_ev, False, *args)
        fill_y(msg_od, True, *args)


def gradient(load):
    near, far = 3.0 / 18.0, 3.0 / 36.0
    mid = load(0, 0)
    up_y, down_y, up_z, down_z = load(1, 0), load(-1, 0), load(0, 1), load(0, -1)
    pp, pm, mp, mm = load(1, 1), load(1, -1), load(-1, 1), load(-1, -1)
    along_x = near * mid + far * ((up_y + down_y) + (up_z + down_z))
    diff_y = up_y - down_y
    diff_z = up_z - down_z
    cross = pp - mm
    other = pm - mp
    grad_x = rolled(along_x, -1) - rolled(along_x, 1)
    grad_y = near * diff_y + far * ((cross + other) + (rolled(diff_y, 1) + rolled(diff_y, -1)))
    grad_z = near * diff_z + far * ((cross - other) + (rolled(diff_z, 1) + rolled(diff_z, -1)))
    return grad_x, grad_y, grad_z


def collide(level, rest_level, tensor, flow, grad, h, share, tail, store_post, store_red):
    def emit(c, post, odd):
        i = INDEX[c]
        if tail is not None:
            post = post + tail[i]
        red = share * post
        if odd is not None:
            red = red + odd
        store_post(i, post)
        store_red(i, red)

    emit((0, 0, 0), rest_level, None)
    xx, yy, zz, xy, xz, yz = tensor
    diag = (xx, yy, zz)
    lev = [level + d for d in diag]
    step = [h * g for g in grad]
    for axis in range(3):
        even = lev[axis] + lev[axis]
        odd = flow[axis] + flow[axis]
        recolour = step[axis] + step[axis]
        c = [0, 0, 0]
        c[axis] = 1
        emit(tuple(c), even + odd, recolour)
        c[axis] = -1
        emit(tuple(c), even - odd, -recolour)
    slant = [s * (1.0 / math.sqrt(2.0)) for s in step]
    for a, b, cross in ((0, 1, xy), (0, 2, xz), (1, 2, yz)):
        base = lev[a] + diag[b]
        twice = cross + cross
        for sign in (1, -1):
            even = base + twice if sign > 0 else base - twice
            odd = flow[a] + flow[b] if sign > 0 else flow[a] - flow[b]
            recolour = slant[a] + slant[b] if sign > 0 else slant[a] - slant[b]
            c = [0, 0, 0]
            c[a], c[b] = 1, sign
            emit(tuple(c), even + odd, recolour)
            emit(tuple(-v for v in c), even - odd, -recolour)


def surface(grad):
    square = grad[0] * grad[0] + grad[1] * grad[1] + grad[2] * grad[2]
    root = lax.rsqrt(jnp.maximum(square, 1e-30))
    return square * root, jnp.minimum(root, 1.0 / grad_floor)


W2 = 1.0 / 36.0


def products(vec, other):
    x, y, z = vec
    p, q, r = other
    return [x * p, y * q, z * r, x * q, x * r, y * r]


def step_one(label, dens, vel, grad, store_post, store_red):
    rho_red = label * dens
    rho_blue = (1.0 - label) * dens
    mix = rho_red * rho_blue / dens
    gmag, inv = surface(grad)
    speed = vel[0] * vel[0] + vel[1] * vel[1] + vel[2] * vel[2]
    scaled = W2 * dens

    def relax(pop, eq):
        return pop - (pop - eq) * (1.0 / relax_time)

    rest = scaled - 1.5 * scaled * speed
    rest = relax(rest, rest)
    flow = [3.0 * scaled * v for v in vel]
    flow = [relax(v, v) for v in flow]
    wide = [(1.5 * f) for f in flow]
    tensor = products(wide, vel)
    pull = (0.5 * surface_amp * W2) * inv
    tensor = [t + s for t, s in zip(tensor, products([pull * g for g in grad], grad))]
    gm = (0.5 * surface_amp * W2) * gmag
    collide(rest - gm, 12.0 * (rest + gm), tensor, flow, grad, (recolouring_strength * W2) * mix * inv, label, None, store_post, store_red)


def step_two(rho, rho_red, pops, grad, store_post, store_red):
    rinv = 1.0 / rho
    share = rho_red * rinv
    mix = share * (rho - rho_red)
    gmag, inv = surface(grad)

    def mom(a):
        total = None
        for i, c in enumerate(VELOCITIES):
            if c[a]:
                term = pops[i]
                total = (term if c[a] > 0 else -term) if total is None else (total + term if c[a] > 0 else total - term)
        return total

    gain = 1.0 / relax_time
    moment = [mom(a) for a in range(3)]
    vel = [m * rinv for m in moment]
    flow = [(3.0 * gain * W2) * m for m in moment]
    half = [1.5 * f for f in flow]
    tensor = products(half, vel)
    rest = (gain * W2) * rho - (1.0 / 3.0) * (tensor[0] + tensor[1] + tensor[2])
    pull = (0.5 * surface_amp * W2) * inv
    tensor = [t + s for t, s in zip(tensor, products([pull * g for g in grad], grad))]
    gm = (0.5 * surface_amp * W2) * gmag
    tail = [(1.0 - gain) * p for p in pops]
    collide(rest - gm, 12.0 * (rest + gm), tensor, flow, grad, (recolouring_strength * W2) * mix * inv, share, tail, store_post, store_red)


def streamed_sum(load, weight=None):
    parts = {0: None, 1: None, -1: None}
    for i, c in enumerate(VELOCITIES):
        w = 1 if weight is None else c[weight]
        if not w:
            continue
        term = load(i)
        held = parts[c[0]]
        parts[c[0]] = (term if w > 0 else -term) if held is None else (held + term if w > 0 else held - term)
    return parts


def compute(phase, density, velocity, z_ev, z_od, y_ev, y_od, out_red, out_blue, out_mom, sign, raw, post1, red1, rho_s, red_s, col_s, post2, red2):
    odd_z = lax.rem(lax.axis_index("gz"), 2) == 1
    odd_y = lax.rem(lax.axis_index("gy"), 2) == 1

    def assemble(row, y):
        for at in range(5):
            ref = sign if at == 4 else raw.at[at]
            ref[row, 4:20, :] = own_plane(at, y, phase, density, velocity)

            @pl.when(odd_z)
            def _():
                put_z_halo(ref, row, at, z_ev, y, False)
                put_z_halo(ref, row, at, z_od, y, True)

            @pl.when(jnp.logical_not(odd_z))
            def _():
                put_z_halo(ref, row, at, z_od, y, False)
                put_z_halo(ref, row, at, z_ev, y, True)

    def assemble_body(y, carry):
        assemble(y + 4, y)
        return carry

    lax.fori_loop(0, 16, assemble_body, 0)

    def take(low, high):
        for at in range(5):
            ref = sign if at == 4 else raw.at[at]
            count = 4 if at == 4 else 3
            for k in range(count):
                ref[4 - count + k, 0:24, :] = low[3 * at + k]
                ref[20 + k, 0:24, :] = high[3 * at + k]

    @pl.when(odd_y)
    def _():
        take(y_ev, y_od)

    @pl.when(jnp.logical_not(odd_y))
    def _():
        take(y_od, y_ev)

    def pass_a(j, carry):
        for k in (0, 8, 16):
            lab = lambda dy, dz: 2.0 * sign[j + 1 + dy, 1 + dz + k : 9 + dz + k, :] - 1.0
            grad = gradient(lab)
            tile = lambda at: raw[at, j + 1, 1 + k : 9 + k, :]

            def store_post(i, v):
                post1[i, j, k : k + 8, :] = v

            def store_red(i, v):
                red1[i, j, k : k + 8, :] = v

            step_one(sign[j + 1, 1 + k : 9 + k, :], tile(0), [tile(1), tile(2), tile(3)], grad, store_post, store_red)
        return carry

    lax.fori_loop(0, 22, pass_a, 0)

    def pass_b(j, carry):
        for k in (0, 8, 16):

            def total(ref):
                def load(i):
                    _, cy, cz = VELOCITIES[i]
                    return ref[i, j + 1 - cy, 1 - cz + k : 9 - cz + k, :]

                parts = streamed_sum(load)
                return parts[0] + (rolled(parts[1], 1) + rolled(parts[-1], -1))

            rho = total(post1)
            red = total(red1)
            rho_s[j, k : k + 8, :] = rho
            red_s[j, k : k + 8, :] = red
            col_s[j, k : k + 8, :] = (red - (rho - red)) / rho
        return carry

    lax.fori_loop(0, 20, pass_b, 0)

    def pass_c(j, carry):
        for k in (0, 8, 16):
            pops = []
            for i, (cx, cy, cz) in enumerate(VELOCITIES):
                pops.append(rolled(post1[i, j + 2 - cy, 2 - cz + k : 10 - cz + k, :], cx))
            grad = gradient(lambda dy, dz: col_s[j + 1 + dy, 1 + dz + k : 9 + dz + k, :])

            def store_post(i, v):
                post2[i, j, k : k + 8, :] = v

            def store_red(i, v):
                red2[i, j, k : k + 8, :] = v

            step_two(rho_s[j + 1, 1 + k : 9 + k, :], red_s[j + 1, 1 + k : 9 + k, :], pops, grad, store_post, store_red)
        return carry

    lax.fori_loop(0, 18, pass_c, 0)

    def pass_d(j, carry):
        for k in (0, 8):

            def load_of(ref):
                def load(i):
                    _, cy, cz = VELOCITIES[i]
                    return ref[i, j + 1 - cy, 1 - cz + k : 9 - cz + k, :]

                return load

            pops = {}

            def load(i):
                if i not in pops:
                    pops[i] = load_of(post2)(i)
                return pops[i]

            def joined(parts):
                side = rolled(parts[1], 1) + rolled(parts[-1], -1)
                return side if parts[0] is None else parts[0] + side

            parts = streamed_sum(load)
            up, down = rolled(parts[1], 1), rolled(parts[-1], -1)
            rho = parts[0] + (up + down)
            red = joined(streamed_sum(load_of(red2)))
            out_red[j, k : k + 8, :] = red
            out_blue[j, k : k + 8, :] = rho - red
            out_mom[0, j, k : k + 8, :] = up - down
            out_mom[1, j, k : k + 8, :] = joined(streamed_sum(load, 1))
            out_mom[2, j, k : k + 8, :] = joined(streamed_sum(load, 2))
        return carry

    lax.fori_loop(0, 16, pass_d, 0)


def f32(*shape):
    return jax.ShapeDtypeStruct(shape, jnp.float32)


def swap(value, axis, first):
    count = lax.axis_size(axis)
    pairs = []
    for low in range(first, count, 2):
        high = (low + 1) % count
        pairs += [(low, high), (high, low)]
    return lax.ppermute(value, axis, pairs)


def shards(phase, density, velocity):
    msg_ev, msg_od = pl.pallas_call(pack_z, out_shape=(f32(16, 16, 128),) * 2, compiler_params=VMEM)(phase, density, velocity)
    z_od = swap(msg_od, "gz", 1)
    z_ev = swap(msg_ev, "gz", 0)
    msg_ev, msg_od = pl.pallas_call(pack_y, out_shape=(f32(16, 24, 128),) * 2, compiler_params=VMEM)(phase, density, velocity, z_ev, z_od)
    y_od = swap(msg_od, "gy", 1)
    y_ev = swap(msg_ev, "gy", 0)
    scratch = [
        pltpu.VMEM((24, 32, 128), jnp.float32),
        pltpu.VMEM((4, 24, 32, 128), jnp.float32),
        pltpu.VMEM((19, 22, 32, 128), jnp.float32),
        pltpu.VMEM((19, 22, 32, 128), jnp.float32),
        pltpu.VMEM((20, 32, 128), jnp.float32),
        pltpu.VMEM((20, 32, 128), jnp.float32),
        pltpu.VMEM((20, 32, 128), jnp.float32),
        pltpu.VMEM((19, 18, 24, 128), jnp.float32),
        pltpu.VMEM((19, 18, 24, 128), jnp.float32),
    ]
    return pl.pallas_call(
        compute,
        out_shape=(f32(16, 16, 128), f32(16, 16, 128), f32(3, 16, 16, 128)),
        scratch_shapes=scratch,
        compiler_params=VMEM,
    )(phase, density, velocity, z_ev, z_od, y_ev, y_od)


def solution(mesh):
    placed = (P("gy", "gz", None), P("gy", "gz", None), P(None, "gy", "gz", None))
    return jax.shard_map(
        shards,
        mesh=mesh,
        in_specs=placed,
        out_specs=placed,
        check_vma=False,
    )
```

```python
import math

import jax
import jax.numpy as jnp
from jax import lax
from jax.experimental import pallas as pl
from jax.experimental.pallas import tpu as pltpu
from jax.sharding import PartitionSpec as P

VELOCITIES = [
    [0, 0, 0],
    [1, 0, 0],
    [-1, 0, 0],
    [0, 1, 0],
    [0, -1, 0],
    [0, 0, 1],
    [0, 0, -1],
    [1, 1, 0],
    [-1, -1, 0],
    [1, -1, 0],
    [-1, 1, 0],
    [1, 0, 1],
    [-1, 0, -1],
    [1, 0, -1],
    [-1, 0, 1],
    [0, 1, 1],
    [0, -1, -1],
    [0, 1, -1],
    [0, -1, 1],
]
INDEX = {tuple(v): i for i, v in enumerate(VELOCITIES)}
relax_time = 0.8
surface_amp = 0.05
recolouring_strength = 0.7
grad_floor = 0.05


def vmem(mib):
    return pltpu.CompilerParams(vmem_limit_bytes=mib * 1024 * 1024)


def rolled(value, shift):
    return pltpu.roll(value, shift % 128, 1) if shift else value


def depth(at):
    return 4 if at == 4 else 3


def fill_z(msg, low, phase, density, velocity):
    for at in range(5):
        n = depth(at)
        start = 0 if low else 16 - n
        if at == 0:
            msg[:, 0:3, :] = density[:, start : start + n, :]
        elif at == 4:
            msg[:, 12:16, :] = phase[:, start : start + n, :].astype(jnp.float32)
        else:
            msg[:, 3 * at : 3 * at + n, :] = velocity[at - 1, :, start : start + n, :]


def fill_y(msg, low, phase, density, velocity):
    for at in range(5):
        for k in range(depth(at)):
            y = k if low else 16 - depth(at) + k
            msg[3 * at + k] = own_plane(at, y, phase, density, velocity)


def own_plane(at, y, phase, density, velocity):
    if at == 0:
        return density[y]
    if at == 4:
        return phase[y].astype(jnp.float32)
    return velocity[at - 1, y]


def is_odd(axis):
    return lax.rem(lax.axis_index(axis), 2) == 1


def either(odd, work):
    @pl.when(odd)
    def _():
        work(True)

    @pl.when(jnp.logical_not(odd))
    def _():
        work(False)


def pack_own(phase_in, density_in, velocity_in, phase, density, velocity, z_ev, z_od, y_ev, y_od, sems):
    copies = [
        pltpu.make_async_copy(velocity_in, velocity, sems.at[0]),
        pltpu.make_async_copy(density_in, density, sems.at[1]),
        pltpu.make_async_copy(phase_in, phase, sems.at[2]),
    ]
    for c in copies:
        c.start()
    for c in copies:
        c.wait()
    own = (phase, density, velocity)

    def along_z(odd):
        fill_z(z_ev, odd, *own)
        fill_z(z_od, not odd, *own)

    def along_y(odd):
        fill_y(y_ev, odd, *own)
        fill_y(y_od, not odd, *own)

    either(is_odd("gz"), along_z)
    either(is_odd("gy"), along_y)


def pack_corners(from_ev, from_od, msg_ev, msg_od):
    odd_y = is_odd("gy")

    def fill(msg, low, z_low, z_high):
        for at in range(5):
            n = depth(at)
            for k in range(n):
                y = k if low else 16 - n + k
                row = 3 * at + k
                if n == 3:
                    msg[row] = jnp.zeros((8, 128), jnp.float32)
                msg[row, 4 - n : 4, :] = z_low[y, 3 * at : 3 * at + n, :]
                msg[row, 4 : 4 + n, :] = z_high[y, 3 * at : 3 * at + n, :]

    def along_z(odd_z):
        z_low, z_high = (from_ev, from_od) if odd_z else (from_od, from_ev)

        def along_y(odd):
            fill(msg_ev, odd, z_low, z_high)
            fill(msg_od, not odd, z_low, z_high)

        either(odd_y, along_y)

    either(is_odd("gz"), along_z)


W2 = 1.0 / 36.0
GAIN = 1.0 / relax_time
LEFT = 1.0 - GAIN


def gradient(load):
    near, far = 6.0 / 18.0, 6.0 / 36.0
    mid = load(0, 0)
    up_y, down_y, up_z, down_z = load(1, 0), load(-1, 0), load(0, 1), load(0, -1)
    pp, pm, mp, mm = load(1, 1), load(1, -1), load(-1, 1), load(-1, -1)
    along_x = near * mid + far * ((up_y + down_y) + (up_z + down_z))
    diff_y = up_y - down_y
    diff_z = up_z - down_z
    cross = pp - mm
    other = pm - mp
    grad_x = rolled(along_x, -1) - rolled(along_x, 1)
    grad_y = near * diff_y + far * ((cross + other) + (rolled(diff_y, 1) + rolled(diff_y, -1)))
    grad_z = near * diff_z + far * ((cross - other) + (rolled(diff_z, 1) + rolled(diff_z, -1)))
    return grad_x, grad_y, grad_z


def collide(level, rest, tensor, flow, step, share, tail, store_post, store_red):
    def emit(c, post, recolour):
        i = INDEX[c]
        if tail is not None:
            post = post + tail[i]
        red = share * post
        if recolour is not None:
            red = red + recolour
        store_post(i, post)
        store_red(i, red)

    emit((0, 0, 0), rest, None)
    xx, yy, zz, xy, xz, yz = tensor
    diag = (xx, yy, zz)
    lev = [level + d for d in diag]
    for axis in range(3):
        even = lev[axis] + lev[axis]
        odd = flow[axis] + flow[axis]
        recolour = step[axis] + step[axis]
        c = [0, 0, 0]
        c[axis] = 1
        emit(tuple(c), even + odd, recolour)
        c[axis] = -1
        emit(tuple(c), even - odd, -recolour)
    slant = [s * (1.0 / math.sqrt(2.0)) for s in step]
    for a, b, cross in ((0, 1, xy), (0, 2, xz), (1, 2, yz)):
        base = lev[a] + diag[b]
        twice = cross + cross
        for sign in (1, -1):
            even = base + twice if sign > 0 else base - twice
            odd = flow[a] + flow[b] if sign > 0 else flow[a] - flow[b]
            recolour = slant[a] + slant[b] if sign > 0 else slant[a] - slant[b]
            c = [0, 0, 0]
            c[a], c[b] = 1, sign
            emit(tuple(c), even + odd, recolour)
            emit(tuple(-v for v in c), even - odd, -recolour)


def surface(grad):
    square = grad[0] * grad[0] + grad[1] * grad[1] + grad[2] * grad[2]
    root = lax.rsqrt(jnp.maximum(square, 1e-30))
    return square * root, jnp.minimum(root, 1.0 / grad_floor)


def products(vec, other):
    x, y, z = vec
    p, q, r = other
    return [x * p, y * q, z * r, x * q, x * r, y * r]


def step_one(label, dens, vel, grad, store_post, store_red):
    scale = LEFT * W2
    mix = label * (1.0 - label) * dens
    gmag, inv = surface(grad)
    speed = vel[0] * vel[0] + vel[1] * vel[1] + vel[2] * vel[2]
    scaled = scale * dens

    def relax(pop, eq):
        return pop - (pop - eq) * GAIN

    rest = scaled - 1.5 * scaled * speed
    rest = relax(rest, rest)
    flow = [(3.0 * scaled) * v for v in vel]
    flow = [relax(v, v) for v in flow]
    tensor = products([1.5 * f for f in flow], vel)
    pull = (0.5 * surface_amp * scale) * inv
    tensor = [t + s for t, s in zip(tensor, products([pull * g for g in grad], grad))]
    gm = (0.5 * surface_amp * scale) * gmag
    h = (recolouring_strength * scale) * mix * inv
    collide(rest - gm, 12.0 * (rest + gm), tensor, flow, [h * g for g in grad], label, None, store_post, store_red)


def moment(pops, a):
    total = None
    for i, c in enumerate(VELOCITIES):
        if c[a]:
            term = pops[i]
            total = (term if c[a] > 0 else -term) if total is None else (total + term if c[a] > 0 else total - term)
    return total


def step_two(rho, rinv, share, tail, grad, store_post, store_red):
    mix = share * (1.0 - share) * rho
    gmag, inv = surface(grad)
    scaled = [moment(tail, a) for a in range(3)]
    vel = [(rinv * (1.0 / LEFT)) * m for m in scaled]
    flow = [(3.0 * GAIN * W2 / LEFT) * m for m in scaled]
    tensor = products([1.5 * f for f in flow], vel)
    rest = (GAIN * W2) * rho - (1.0 / 3.0) * (tensor[0] + tensor[1] + tensor[2])
    pull = (0.5 * surface_amp * W2) * inv
    tensor = [t + s for t, s in zip(tensor, products([pull * g for g in grad], grad))]
    gm = (0.5 * surface_amp * W2) * gmag
    h = (recolouring_strength * W2) * mix * inv
    collide(rest - gm, 12.0 * (rest + gm), tensor, flow, [h * g for g in grad], share, tail, store_post, store_red)


def streamed_parts(load, weight=None):
    parts = {0: [], 1: [], -1: []}
    for i, c in enumerate(VELOCITIES):
        w = 1 if weight is None else c[weight]
        if w:
            parts[c[0]].append((load(i), w))

    def tree(terms):
        while len(terms) > 1:
            joined = []
            for (a, wa), (b, wb) in zip(terms[::2], terms[1::2]):
                if wa == wb:
                    joined.append((a + b, wa))
                elif wa > 0:
                    joined.append((a - b, 1))
                else:
                    joined.append((b - a, 1))
            terms = joined + terms[len(terms) & ~1 :]
        value, w = terms[0]
        return value if w > 0 else -value

    return {s: tree(terms) if terms else None for s, terms in parts.items()}


def joined(parts):
    side = rolled(parts[1], 1) + rolled(parts[-1], -1)
    return side if parts[0] is None else parts[0] + side


def pass_a(refs, j, k):
    label, raw, post1, red1 = refs["label"], refs["raw"], refs["post1"], refs["red1"]
    grad = gradient(lambda dy, dz: label[j + 1 + dy, 1 + dz + k : 9 + dz + k, :])
    tile = lambda at: raw[at, j + 1, 1 + k : 9 + k, :]

    def store_post(i, v):
        post1[i, j, k : k + 8, :] = v

    def store_red(i, v):
        red1[i, j, k : k + 8, :] = v

    step_one(label[j + 1, 1 + k : 9 + k, :], tile(0), [tile(1), tile(2), tile(3)], grad, store_post, store_red)


def pass_b(refs, j, k):
    def total(ref):
        def load(i):
            _, cy, cz = VELOCITIES[i]
            return ref[i, j + 1 - cy, 1 - cz + k : 9 - cz + k, :]

        return joined(streamed_parts(load)) * (1.0 / LEFT)

    rho = total(refs["post1"])
    rinv = 1.0 / rho
    refs["rho_s"][j, k : k + 8, :] = rho
    refs["rinv_s"][j, k : k + 8, :] = rinv
    refs["share_s"][j, k : k + 8, :] = total(refs["red1"]) * rinv


def pass_c(refs, j, k):
    post1, post2, red2, share = refs["post1"], refs["post2"], refs["red2"], refs["share_s"]
    tail = []
    for i, (cx, cy, cz) in enumerate(VELOCITIES):
        tail.append(rolled(post1[i, j + 2 - cy, 2 - cz + k : 10 - cz + k, :], cx))
    grad = gradient(lambda dy, dz: share[j + 1 + dy, 1 + dz + k : 9 + dz + k, :])
    tile = lambda ref: ref[j + 1, 1 + k : 9 + k, :]

    def store_post(i, v):
        post2[i, j, k : k + 8, :] = v

    def store_red(i, v):
        red2[i, j, k : k + 8, :] = v

    step_two(tile(refs["rho_s"]), tile(refs["rinv_s"]), tile(share), tail, grad, store_post, store_red)


def pass_d(refs, j, k, store):
    def load_of(ref):
        held = {}

        def load(i):
            if i not in held:
                _, cy, cz = VELOCITIES[i]
                held[i] = ref[i, j + 1 - cy, 1 - cz + k : 9 - cz + k, :]
            return held[i]

        return load

    load = load_of(refs["post2"])
    parts = streamed_parts(load)
    up, down = rolled(parts[1], 1), rolled(parts[-1], -1)
    rho = parts[0] + (up + down)
    red = joined(streamed_parts(load_of(refs["red2"])))
    store(j, k, [red, rho - red, up - down, joined(streamed_parts(load, 1)), joined(streamed_parts(load, 2))])


def sweep(work, refs, rows, chunks, unroll):
    count = rows[0][1] - rows[0][0]

    def body(t, carry):
        for start, _ in rows:
            for k in chunks:
                work(refs, start + t, k)
        return carry

    lax.fori_loop(0, count, body, 0, unroll=unroll)


STATE = dict(
    label=(24, 32, 128),
    raw=(4, 24, 32, 128),
    post1=(19, 22, 32, 128),
    red1=(19, 22, 32, 128),
    rho_s=(20, 32, 128),
    rinv_s=(20, 32, 128),
    share_s=(20, 32, 128),
    post2=(19, 18, 24, 128),
    red2=(19, 18, 24, 128),
)
NAMES = list(STATE)
A_Z, B_Z, C_Z, D_Z = (0, 8, 16), (0, 8, 14), (0, 8, 12), (0, 8)


def frame_of(refs, at):
    return refs["label"] if at == 4 else refs["raw"].at[at]


def inner(phase, density, velocity, z_ev, z_od, y_ev, y_od, *rest):
    refs = dict(zip(NAMES, rest))
    done = rest[len(NAMES)]

    def assemble(odd):
        low, high = (z_ev, z_od) if odd else (z_od, z_ev)

        def body(y, carry):
            for at in range(5):
                ref, n = frame_of(refs, at), depth(at)
                ref[y + 4, 4:20, :] = own_plane(at, y, phase, density, velocity)
                ref[y + 4, 4 - n : 4, :] = low[y, 3 * at : 3 * at + n, :]
                ref[y + 4, 20 : 20 + n, :] = high[y, 3 * at : 3 * at + n, :]
            return carry

        lax.fori_loop(0, 16, body, 0, unroll=2)

    def beside(odd):
        low, high = (y_ev, y_od) if odd else (y_od, y_ev)
        for at in range(5):
            ref, n = frame_of(refs, at), depth(at)
            for k in range(n):
                ref[4 - n + k, 4:20, :] = low[3 * at + k]
                ref[20 + k, 4:20, :] = high[3 * at + k]

    either(is_odd("gz"), assemble)
    either(is_odd("gy"), beside)

    def store(j, k, values):
        for at, v in enumerate(values):
            done[at, j - 4, k : k + 8, :] = v

    sweep(pass_a, refs, [(4, 18)], A_Z, 2)
    sweep(pass_a, refs, [(0, 4), (18, 22)], A_Z[1:2], 2)
    sweep(pass_b, refs, [(4, 16)], B_Z, 2)
    sweep(pass_b, refs, [(0, 4), (16, 20)], B_Z[1:2], 2)
    sweep(pass_c, refs, [(4, 14)], C_Z, 2)
    sweep(pass_c, refs, [(0, 4), (14, 18)], C_Z[1:2], 2)
    sweep(lambda r, j, k: pass_d(r, j, k, store), refs, [(4, 12)], D_Z, 2)


def outer(y_ev, y_od, done, *rest):
    n = len(NAMES)
    refs = dict(zip(NAMES, rest[n : 2 * n]))
    out_red, out_blue, out_mom, edge, sems = rest[2 * n :]

    def send(src, rows, at_rows, sem):
        outs = [out_red, out_blue, out_mom.at[0], out_mom.at[1], out_mom.at[2]]
        return [pltpu.make_async_copy(src.at[f, pl.ds(rows, at_rows[1])], outs[f].at[pl.ds(at_rows[0], at_rows[1])], sems.at[sem, f]) for f in range(5)]

    first = send(done, 0, (4, 8), 0)
    for c in first:
        c.start()

    def corners(odd):
        low, high = (y_ev, y_od) if odd else (y_od, y_ev)
        for at in range(5):
            ref, d = frame_of(refs, at), depth(at)
            for k in range(d):
                for row, msg in ((4 - d + k, low), (20 + k, high)):
                    ref[row, 4 - d : 4, :] = msg[3 * at + k, 4 - d : 4, :]
                    ref[row, 20 : 20 + d, :] = msg[3 * at + k, 4 : 4 + d, :]

    either(is_odd("gy"), corners)

    def store_low(j, k, values):
        for at, v in enumerate(values):
            edge[at, j, k : k + 8, :] = v

    def store_high(j, k, values):
        for at, v in enumerate(values):
            edge[at, j - 8, k : k + 8, :] = v

    sweep(pass_a, refs, [(0, 4), (18, 22)], A_Z[::2], 2)
    sweep(pass_b, refs, [(0, 4), (16, 20)], B_Z[::2], 2)
    sweep(pass_c, refs, [(0, 4), (14, 18)], C_Z[::2], 2)

    def last(r, t, k):
        pass_d(r, t, k, store_low)
        pass_d(r, t + 12, k, store_high)

    sweep(last, refs, [(0, 4)], D_Z, 2)
    second = send(edge, 0, (0, 4), 1) + send(edge, 4, (12, 4), 2)
    for c in second:
        c.start()
    for c in first + second:
        c.wait()


def f32(*shape):
    return jax.ShapeDtypeStruct(shape, jnp.float32)


def swap(value, axis, first):
    count = lax.axis_size(axis)
    pairs = []
    for low in range(first, count, 2):
        high = (low + 1) % count
        pairs += [(low, high), (high, low)]
    return lax.ppermute(value, axis, pairs)


def shards(phase, density, velocity):
    in_vmem = pl.BlockSpec(memory_space=pltpu.VMEM)
    in_hbm = pl.BlockSpec(memory_space=pltpu.HBM)
    state = [f32(*s) for s in STATE.values()]
    phase, density, velocity, z_ev, z_od, y_ev, y_od = pl.pallas_call(
        pack_own,
        out_shape=(jax.ShapeDtypeStruct((16, 16, 128), jnp.int32), f32(16, 16, 128), f32(3, 16, 16, 128)) + (f32(16, 16, 128),) * 4,
        in_specs=[in_hbm] * 3,
        out_specs=(in_vmem,) * 7,
        scratch_shapes=[pltpu.SemaphoreType.DMA((3,))],
        compiler_params=vmem(8),
    )(phase, density, velocity)
    z_od = swap(z_od, "gz", 1)
    z_ev = swap(z_ev, "gz", 0)
    y_od = swap(y_od, "gy", 1)
    y_ev = swap(y_ev, "gy", 0)
    c_ev, c_od = pl.pallas_call(pack_corners, out_shape=(f32(16, 8, 128),) * 2, compiler_params=vmem(4))(z_ev, z_od)
    c_od = swap(c_od, "gy", 1)
    c_ev = swap(c_ev, "gy", 0)
    made = pl.pallas_call(
        inner,
        out_shape=tuple(state) + (f32(5, 8, 16, 128),),
        compiler_params=vmem(8),
        cost_estimate=pl.CostEstimate(flops=40_000_000, bytes_accessed=20_000_000, transcendentals=0),
    )(phase, density, velocity, z_ev, z_od, y_ev, y_od)
    n = len(NAMES)
    return pl.pallas_call(
        outer,
        out_shape=tuple(state) + (f32(16, 16, 128), f32(16, 16, 128), f32(3, 16, 16, 128)),
        in_specs=[in_vmem] * (3 + n),
        out_specs=(in_vmem,) * n + (in_hbm,) * 3,
        scratch_shapes=[pltpu.VMEM((5, 8, 16, 128), jnp.float32), pltpu.SemaphoreType.DMA((3, 5))],
        input_output_aliases={3 + i: i for i in range(n)},
        compiler_params=vmem(8),
    )(c_ev, c_od, made[n], *made[:n])[n:]


def solution(mesh):
    placed = (P("gy", "gz", None), P("gy", "gz", None), P(None, "gy", "gz", None))
    return jax.shard_map(
        shards,
        mesh=mesh,
        in_specs=placed,
        out_specs=placed,
        check_vma=False,
    )
```

```python
import math

import jax
import jax.numpy as jnp
from jax import lax
from jax.experimental import pallas as pl
from jax.experimental.pallas import tpu as pltpu
from jax.sharding import PartitionSpec as P

VELOCITIES = [
    [0, 0, 0],
    [1, 0, 0],
    [-1, 0, 0],
    [0, 1, 0],
    [0, -1, 0],
    [0, 0, 1],
    [0, 0, -1],
    [1, 1, 0],
    [-1, -1, 0],
    [1, -1, 0],
    [-1, 1, 0],
    [1, 0, 1],
    [-1, 0, -1],
    [1, 0, -1],
    [-1, 0, 1],
    [0, 1, 1],
    [0, -1, -1],
    [0, 1, -1],
    [0, -1, 1],
]
INDEX = {tuple(v): i for i, v in enumerate(VELOCITIES)}
relax_time = 0.8
surface_amp = 0.05
recolouring_strength = 0.7
grad_floor = 0.05


def vmem(mib):
    return pltpu.CompilerParams(vmem_limit_bytes=mib * 1024 * 1024)


def rolled(value, shift):
    return pltpu.roll(value, shift % 128, 1) if shift else value


def depth(at):
    return 4 if at == 4 else 3


def fill_z(msg, low, phase, density, velocity):
    for at in range(5):
        n = depth(at)
        start = 0 if low else 16 - n
        if at == 0:
            msg[:, 0:3, :] = density[:, start : start + n, :]
        elif at == 4:
            msg[:, 12:16, :] = phase[:, start : start + n, :].astype(jnp.float32)
        else:
            msg[:, 3 * at : 3 * at + n, :] = velocity[at - 1, :, start : start + n, :]


def fill_y(msg, low, phase, density, velocity):
    for at in range(5):
        for k in range(depth(at)):
            y = k if low else 16 - depth(at) + k
            msg[3 * at + k] = own_plane(at, y, phase, density, velocity)


def own_plane(at, y, phase, density, velocity):
    if at == 0:
        return density[y]
    if at == 4:
        return phase[y].astype(jnp.float32)
    return velocity[at - 1, y]


def is_odd(axis):
    return lax.rem(lax.axis_index(axis), 2) == 1


def either(odd, work):
    @pl.when(odd)
    def _():
        work(True)

    @pl.when(jnp.logical_not(odd))
    def _():
        work(False)


def pack_own(phase_in, density_in, velocity_in, phase, density, velocity, z_ev, z_od, y_ev, y_od, sems):
    copies = [
        pltpu.make_async_copy(velocity_in, velocity, sems.at[0]),
        pltpu.make_async_copy(density_in, density, sems.at[1]),
        pltpu.make_async_copy(phase_in, phase, sems.at[2]),
    ]
    for c in copies:
        c.start()
    for c in copies:
        c.wait()
    own = (phase, density, velocity)

    def along_z(odd):
        fill_z(z_ev, odd, *own)
        fill_z(z_od, not odd, *own)

    def along_y(odd):
        fill_y(y_ev, odd, *own)
        fill_y(y_od, not odd, *own)

    either(is_odd("gz"), along_z)
    either(is_odd("gy"), along_y)


def pack_corners(from_ev, from_od, msg_ev, msg_od):
    odd_y = is_odd("gy")

    def fill(msg, low, z_low, z_high):
        for at in range(5):
            n = depth(at)
            for k in range(n):
                y = k if low else 16 - n + k
                row = 3 * at + k
                if n == 3:
                    msg[row] = jnp.zeros((8, 128), jnp.float32)
                msg[row, 4 - n : 4, :] = z_low[y, 3 * at : 3 * at + n, :]
                msg[row, 4 : 4 + n, :] = z_high[y, 3 * at : 3 * at + n, :]

    def along_z(odd_z):
        z_low, z_high = (from_ev, from_od) if odd_z else (from_od, from_ev)

        def along_y(odd):
            fill(msg_ev, odd, z_low, z_high)
            fill(msg_od, not odd, z_low, z_high)

        either(odd_y, along_y)

    either(is_odd("gz"), along_z)


W2 = 1.0 / 36.0
GAIN = 1.0 / relax_time
LEFT = 1.0 - GAIN


def gradient(q):
    near, far = 6.0 / 18.0, 6.0 / 36.0
    mid = q[0, 0]
    up_y, down_y, up_z, down_z = q[1, 0], q[-1, 0], q[0, 1], q[0, -1]
    pp, pm, mp, mm = q[1, 1], q[1, -1], q[-1, 1], q[-1, -1]
    along_x = near * mid + far * ((up_y + down_y) + (up_z + down_z))
    diff_y = up_y - down_y
    diff_z = up_z - down_z
    cross = pp - mm
    other = pm - mp
    grad_x = rolled(along_x, -1) - rolled(along_x, 1)
    grad_y = near * diff_y + far * ((cross + other) + (rolled(diff_y, 1) + rolled(diff_y, -1)))
    grad_z = near * diff_z + far * ((cross - other) + (rolled(diff_z, 1) + rolled(diff_z, -1)))
    return grad_x, grad_y, grad_z


def collide(level, rest, tensor, flow, step, share, tail):
    def left(c, post):
        return post if tail is None else post + tail[INDEX[c]]

    def pair(c, even, odd, recolour):
        back = tuple(-v for v in c)
        post = left(c, even + odd)
        yield INDEX[c], post, share * post + recolour
        post = left(back, even - odd)
        yield INDEX[back], post, share * post - recolour

    post = left((0, 0, 0), rest)
    yield 0, post, share * post
    xx, yy, zz, xy, xz, yz = tensor
    diag = (xx, yy, zz)
    lev = [level + d for d in diag]
    for axis in range(3):
        c = tuple(int(a == axis) for a in range(3))
        yield from pair(c, lev[axis] + lev[axis], flow[axis] + flow[axis], step[axis] + step[axis])
    slant = [s * (1.0 / math.sqrt(2.0)) for s in step]
    for a, b, cross in ((0, 1, xy), (0, 2, xz), (1, 2, yz)):
        base = lev[a] + diag[b]
        twice = cross + cross
        c = tuple(int(v in (a, b)) for v in range(3))
        yield from pair(c, base + twice, flow[a] + flow[b], slant[a] + slant[b])
        c = tuple(int(v == a) - int(v == b) for v in range(3))
        yield from pair(c, base - twice, flow[a] - flow[b], slant[a] - slant[b])


def surface(grad):
    square = grad[0] * grad[0] + grad[1] * grad[1] + grad[2] * grad[2]
    root = lax.rsqrt(jnp.maximum(square, 1e-30))
    return square * root, jnp.minimum(root, 1.0 / grad_floor)


def products(vec, other):
    x, y, z = vec
    p, q, r = other
    return [x * p, y * q, z * r, x * q, x * r, y * r]


def step_one(label, dens, vel, grad):
    scale = LEFT * W2
    mix = label * (1.0 - label) * dens
    gmag, inv = surface(grad)
    speed = vel[0] * vel[0] + vel[1] * vel[1] + vel[2] * vel[2]
    scaled = scale * dens

    def relax(pop, eq):
        return pop - (pop - eq) * GAIN

    rest = scaled - 1.5 * scaled * speed
    rest = relax(rest, rest)
    flow = [(3.0 * scaled) * v for v in vel]
    flow = [relax(v, v) for v in flow]
    tensor = products([1.5 * f for f in flow], vel)
    pull = (0.5 * surface_amp * scale) * inv
    tensor = [t + s for t, s in zip(tensor, products([pull * g for g in grad], grad))]
    gm = (0.5 * surface_amp * scale) * gmag
    h = (recolouring_strength * scale) * mix * inv
    return collide(rest - gm, 12.0 * (rest + gm), tensor, flow, [h * g for g in grad], label, None)


def moment(pops, a):
    total = None
    for i, c in enumerate(VELOCITIES):
        if c[a]:
            term = pops[i]
            total = (term if c[a] > 0 else -term) if total is None else (total + term if c[a] > 0 else total - term)
    return total


def step_two(rho, rinv, share, tail, grad):
    mix = share * (1.0 - share) * rho
    gmag, inv = surface(grad)
    scaled = [moment(tail, a) for a in range(3)]
    vel = [(rinv * (1.0 / LEFT)) * m for m in scaled]
    flow = [(3.0 * GAIN * W2 / LEFT) * m for m in scaled]
    tensor = products([1.5 * f for f in flow], vel)
    rest = (GAIN * W2) * rho - (1.0 / 3.0) * (tensor[0] + tensor[1] + tensor[2])
    pull = (0.5 * surface_amp * W2) * inv
    tensor = [t + s for t, s in zip(tensor, products([pull * g for g in grad], grad))]
    gm = (0.5 * surface_amp * W2) * gmag
    h = (recolouring_strength * W2) * mix * inv
    return collide(rest - gm, 12.0 * (rest + gm), tensor, flow, [h * g for g in grad], share, tail)


def streamed_parts(values, weight=None):
    parts = {0: [], 1: [], -1: []}
    for i, c in enumerate(VELOCITIES):
        w = 1 if weight is None else c[weight]
        if w:
            parts[c[0]].append((values[i], w))

    def tree(terms):
        while len(terms) > 1:
            joined = []
            for (a, wa), (b, wb) in zip(terms[::2], terms[1::2]):
                if wa == wb:
                    joined.append((a + b, wa))
                elif wa > 0:
                    joined.append((a - b, 1))
                else:
                    joined.append((b - a, 1))
            terms = joined + terms[len(terms) & ~1 :]
        value, w = terms[0]
        return value if w > 0 else -value

    return {s: tree(terms) if terms else None for s, terms in parts.items()}


def joined(parts):
    side = rolled(parts[1], 1) + rolled(parts[-1], -1)
    return side if parts[0] is None else parts[0] + side


def load_a(refs, j, k):
    label, raw = refs["label"], refs["raw"]
    near = {(dy, dz): label[j + 1 + dy, 1 + dz + k : 9 + dz + k, :] for dy in (-1, 0, 1) for dz in (-1, 0, 1)}
    return near, [raw[at, j + 1, 1 + k : 9 + k, :] for at in range(4)]


def pass_a(refs, j, k, loaded):
    near, (dens, *vel) = loaded
    for i, post, red in step_one(near[0, 0], dens, vel, gradient(near)):
        yield refs["post1"].at[i], j, k, post
        yield refs["red1"].at[i], j, k, red


def load_b(refs, j, k):
    out = []
    for name in ("post1", "red1"):
        ref = refs[name]
        out.append([ref[i, j + 1 - cy, 1 - cz + k : 9 - cz + k, :] for i, (_, cy, cz) in enumerate(VELOCITIES)])
    return out


def pass_b(refs, j, k, loaded):
    rho, red = [joined(streamed_parts(v)) * (1.0 / LEFT) for v in loaded]
    rinv = 1.0 / rho
    yield refs["rho_s"], j, k, rho
    yield refs["rinv_s"], j, k, rinv
    yield refs["share_s"], j, k, red * rinv


def load_c(refs, j, k):
    post1, share = refs["post1"], refs["share_s"]
    tail = [rolled(post1[i, j + 2 - cy, 2 - cz + k : 10 - cz + k, :], cx) for i, (cx, cy, cz) in enumerate(VELOCITIES)]
    near = {(dy, dz): share[j + 1 + dy, 1 + dz + k : 9 + dz + k, :] for dy in (-1, 0, 1) for dz in (-1, 0, 1)}
    return tail, near, [refs[name][j + 1, 1 + k : 9 + k, :] for name in ("rho_s", "rinv_s")]


def pass_c(refs, j, k, loaded):
    tail, near, (rho, rinv) = loaded
    for i, post, red in step_two(rho, rinv, near[0, 0], tail, gradient(near)):
        yield refs["post2"].at[i], j, k, post
        yield refs["red2"].at[i], j, k, red


def load_d(refs, j, k):
    out = []
    for name in ("post2", "red2"):
        ref = refs[name]
        out.append([ref[i, j + 1 - cy, 1 - cz + k : 9 - cz + k, :] for i, (_, cy, cz) in enumerate(VELOCITIES)])
    return out


def pass_d(refs, j, k, loaded):
    post, red = loaded
    parts = streamed_parts(post)
    up, down = rolled(parts[1], 1), rolled(parts[-1], -1)
    rho = parts[0] + (up + down)
    red = joined(streamed_parts(red))
    for at, v in enumerate([red, rho - red, up - down, joined(streamed_parts(post, 1)), joined(streamed_parts(post, 2))]):
        yield refs["edge"].at[at], j, k, v


PASSES = dict(a=(load_a, pass_a, 3, False), b=(load_b, pass_b, 1, True), c=(load_c, pass_c, 1, False), d=(load_d, pass_d, 1, True))


def sweep(name, refs, rows, chunks, per, shift=0):
    load, work, group, defer = PASSES[name]
    count = rows[0][1] - rows[0][0]

    def put(ref, j, k, value):
        ref[j - shift, k : k + 8, :] = value

    def trip(t, n):
        tiles = [(start + t + r, k) for r in range(n) for start, _ in rows for k in chunks]
        waiting = []
        for at in range(0, len(tiles), group):
            some = tiles[at : at + group]
            held = [load(refs, j, k) for j, k in some]
            for (j, k), loaded in zip(some, held):
                for item in work(refs, j, k, loaded):
                    if defer:
                        waiting.append(item)
                    else:
                        put(*item)
        for item in waiting:
            put(*item)

    def body(t, carry):
        trip(t * per, per)
        return carry

    lax.fori_loop(0, count // per, body, 0)
    if count % per:
        trip(count - count % per, count % per)


PER = 4
STATE = dict(
    label=(24, 32, 128),
    raw=(4, 24, 32, 128),
    post1=(19, 22, 32, 128),
    red1=(19, 22, 32, 128),
    rho_s=(20, 32, 128),
    rinv_s=(20, 32, 128),
    share_s=(20, 32, 128),
    post2=(19, 18, 24, 128),
    red2=(19, 18, 24, 128),
)
NAMES = list(STATE)
A_Z, B_Z, C_Z, D_Z = (0, 8, 16), (0, 8, 14), (0, 8, 12), (0, 8)


def frame_of(refs, at):
    return refs["label"] if at == 4 else refs["raw"].at[at]


def inner(phase, density, velocity, z_ev, z_od, y_ev, y_od, *rest):
    refs = dict(zip(NAMES, rest))
    done = rest[len(NAMES)]

    def assemble(odd):
        low, high = (z_ev, z_od) if odd else (z_od, z_ev)

        def body(y, carry):
            for at in range(5):
                ref, n = frame_of(refs, at), depth(at)
                ref[y + 4, 4:20, :] = own_plane(at, y, phase, density, velocity)
                ref[y + 4, 4 - n : 4, :] = low[y, 3 * at : 3 * at + n, :]
                ref[y + 4, 20 : 20 + n, :] = high[y, 3 * at : 3 * at + n, :]
            return carry

        lax.fori_loop(0, 16, body, 0, unroll=2)

    def beside(odd):
        low, high = (y_ev, y_od) if odd else (y_od, y_ev)
        for at in range(5):
            ref, n = frame_of(refs, at), depth(at)
            for k in range(n):
                ref[4 - n + k, 4:20, :] = low[3 * at + k]
                ref[20 + k, 4:20, :] = high[3 * at + k]

    either(is_odd("gz"), assemble)
    either(is_odd("gy"), beside)

    refs["edge"] = done
    sweep("a", refs, [(4, 18)], A_Z, PER)
    sweep("a", refs, [(0, 4), (18, 22)], A_Z[1:2], PER)
    sweep("b", refs, [(4, 16)], B_Z, PER)
    sweep("b", refs, [(0, 4), (16, 20)], B_Z[1:2], PER)
    sweep("c", refs, [(4, 14)], C_Z, PER)
    sweep("c", refs, [(0, 4), (14, 18)], C_Z[1:2], PER)
    sweep("d", refs, [(4, 12)], D_Z, PER, shift=4)


def outer(y_ev, y_od, done, *rest):
    n = len(NAMES)
    refs = dict(zip(NAMES, rest[n : 2 * n]))
    out_red, out_blue, out_mom, edge, sems = rest[2 * n :]

    def send(src, rows, at_rows, sem):
        outs = [out_red, out_blue, out_mom.at[0], out_mom.at[1], out_mom.at[2]]
        return [pltpu.make_async_copy(src.at[f, pl.ds(rows, at_rows[1])], outs[f].at[pl.ds(at_rows[0], at_rows[1])], sems.at[sem, f]) for f in range(5)]

    first = send(done, 0, (4, 8), 0)
    for c in first:
        c.start()

    def corners(odd):
        low, high = (y_ev, y_od) if odd else (y_od, y_ev)
        for at in range(5):
            ref, d = frame_of(refs, at), depth(at)
            for k in range(d):
                for row, msg in ((4 - d + k, low), (20 + k, high)):
                    ref[row, 4 - d : 4, :] = msg[3 * at + k, 4 - d : 4, :]
                    ref[row, 20 : 20 + d, :] = msg[3 * at + k, 4 : 4 + d, :]

    either(is_odd("gy"), corners)

    refs["edge"] = edge
    sweep("a", refs, [(0, 4), (18, 22)], A_Z[::2], PER)
    sweep("b", refs, [(0, 4), (16, 20)], B_Z[::2], PER)
    sweep("c", refs, [(0, 4), (14, 18)], C_Z[::2], PER)
    sweep("d", refs, [(0, 4)], D_Z, PER)
    sweep("d", refs, [(12, 16)], D_Z, PER, shift=8)
    second = send(edge, 0, (0, 4), 1) + send(edge, 4, (12, 4), 2)
    for c in second:
        c.start()
    for c in first + second:
        c.wait()


def f32(*shape):
    return jax.ShapeDtypeStruct(shape, jnp.float32)


def swap(value, axis, first):
    count = lax.axis_size(axis)
    pairs = []
    for low in range(first, count, 2):
        high = (low + 1) % count
        pairs += [(low, high), (high, low)]
    return lax.ppermute(value, axis, pairs)


def shards(phase, density, velocity):
    phase, density, velocity = [pltpu.with_memory_space_constraint(v, pltpu.HBM) for v in (phase, density, velocity)]
    in_vmem = pl.BlockSpec(memory_space=pltpu.VMEM)
    in_hbm = pl.BlockSpec(memory_space=pltpu.HBM)
    state = [f32(*s) for s in STATE.values()]
    phase, density, velocity, z_ev, z_od, y_ev, y_od = pl.pallas_call(
        pack_own,
        out_shape=(jax.ShapeDtypeStruct((16, 16, 128), jnp.int32), f32(16, 16, 128), f32(3, 16, 16, 128)) + (f32(16, 16, 128),) * 4,
        in_specs=[in_hbm] * 3,
        out_specs=(in_vmem,) * 7,
        scratch_shapes=[pltpu.SemaphoreType.DMA((3,))],
        compiler_params=vmem(8),
    )(phase, density, velocity)
    z_od = swap(z_od, "gz", 1)
    z_ev = swap(z_ev, "gz", 0)
    y_od = swap(y_od, "gy", 1)
    y_ev = swap(y_ev, "gy", 0)
    c_ev, c_od = pl.pallas_call(pack_corners, out_shape=(f32(16, 8, 128),) * 2, compiler_params=vmem(4))(z_ev, z_od)
    c_od = swap(c_od, "gy", 1)
    c_ev = swap(c_ev, "gy", 0)
    made = pl.pallas_call(
        inner,
        out_shape=tuple(state) + (f32(5, 8, 16, 128),),
        compiler_params=vmem(8),
        cost_estimate=pl.CostEstimate(flops=40_000_000, bytes_accessed=20_000_000, transcendentals=0),
    )(phase, density, velocity, z_ev, z_od, y_ev, y_od)
    n = len(NAMES)
    return pl.pallas_call(
        outer,
        out_shape=tuple(state) + (f32(16, 16, 128), f32(16, 16, 128), f32(3, 16, 16, 128)),
        in_specs=[in_vmem] * (3 + n),
        out_specs=(in_vmem,) * n + (in_hbm,) * 3,
        scratch_shapes=[pltpu.VMEM((5, 8, 16, 128), jnp.float32), pltpu.SemaphoreType.DMA((3, 5))],
        input_output_aliases={3 + i: i for i in range(n)},
        compiler_params=vmem(8),
    )(c_ev, c_od, made[n], *made[:n])[n:]


def solution(mesh):
    placed = (P("gy", "gz", None), P("gy", "gz", None), P(None, "gy", "gz", None))
    return jax.shard_map(
        shards,
        mesh=mesh,
        in_specs=placed,
        out_specs=placed,
        check_vma=False,
    )
```

```python
import functools
import math

import jax
import jax.numpy as jnp
from jax import lax
from jax.experimental import pallas as pl
from jax.experimental.pallas import tpu as pltpu
from jax.sharding import PartitionSpec as P

VELOCITIES = [
    [0, 0, 0],
    [1, 0, 0],
    [-1, 0, 0],
    [0, 1, 0],
    [0, -1, 0],
    [0, 0, 1],
    [0, 0, -1],
    [1, 1, 0],
    [-1, -1, 0],
    [1, -1, 0],
    [-1, 1, 0],
    [1, 0, 1],
    [-1, 0, -1],
    [1, 0, -1],
    [-1, 0, 1],
    [0, 1, 1],
    [0, -1, -1],
    [0, 1, -1],
    [0, -1, 1],
]
INDEX = {tuple(v): i for i, v in enumerate(VELOCITIES)}
relax_time = 0.8
surface_amp = 0.05
recolouring_strength = 0.7
grad_floor = 0.05


def vmem(mib):
    return pltpu.CompilerParams(vmem_limit_bytes=mib * 1024 * 1024)


def rolled(value, shift):
    return pltpu.roll(value, shift % 128, 1) if shift else value


def depth(at):
    return 4 if at == 4 else 3


def fill_z(msg, low, phase, density, velocity):
    for at in range(5):
        n = depth(at)
        start = 0 if low else 16 - n
        if at == 0:
            msg[:, 0:3, :] = density[:, start : start + n, :]
        elif at == 4:
            msg[:, 12:16, :] = phase[:, start : start + n, :].astype(jnp.float32)
        else:
            msg[:, 3 * at : 3 * at + n, :] = velocity[at - 1, :, start : start + n, :]


def fill_y(msg, low, phase, density, velocity):
    for at in range(5):
        for k in range(depth(at)):
            y = k if low else 16 - depth(at) + k
            msg[3 * at + k] = own_plane(at, y, phase, density, velocity)


def own_plane(at, y, phase, density, velocity):
    if at == 0:
        return density[y]
    if at == 4:
        return phase[y].astype(jnp.float32)
    return velocity[at - 1, y]


def is_odd(axis):
    return lax.rem(lax.axis_index(axis), 2) == 1


def either(odd, work):
    @pl.when(odd)
    def _():
        work(True)

    @pl.when(jnp.logical_not(odd))
    def _():
        work(False)


def pack_own(phase_in, density_in, velocity_in, phase, density, velocity, z_ev, z_od, y_od, y_ev, sems):
    copies = [
        pltpu.make_async_copy(velocity_in, velocity, sems.at[0]),
        pltpu.make_async_copy(density_in, density, sems.at[1]),
        pltpu.make_async_copy(phase_in, phase, sems.at[2]),
    ]
    for c in copies:
        c.start()
    for c in copies:
        c.wait()
    own = (phase, density, velocity)

    def along_z(odd):
        fill_z(z_ev, odd, *own)
        fill_z(z_od, not odd, *own)

    def along_y(odd):
        fill_y(y_ev, odd, *own)
        fill_y(y_od, not odd, *own)

    either(is_odd("gz"), along_z)
    either(is_odd("gy"), along_y)


def row_index():
    return lax.broadcasted_iota(jnp.int32, (8, 128), 0)


def take_rows(tile, index):
    return jnp.take_along_axis(tile, index, axis=0)


def fold(low, low_at, high, high_at):
    row = row_index()
    q = lax.shift_right_logical(row, 1)
    odd = lax.rem(row, 2) == 1
    return jnp.where(odd, take_rows(high, high_at(q)), take_rows(low, low_at(q)))


def mirror(at, tile):
    return jnp.where(lax.rem(row_index(), 2) == 1, -tile, tile) if at == 3 else tile


def fold_halo(at, low, high, y):
    start, off = (8, 4) if at == 4 else (8, 1) if at == 3 else (3 * at, 0)
    n = depth(at)
    low, high = low[y, start : start + 8, :], high[y, start : start + 8, :]
    return mirror(at, fold(low, lambda q: off + jnp.maximum(q - (4 - n), 0), high, lambda q: off + jnp.minimum(3 - q, n - 1)))


def fold_own(at, plane):
    low, high = plane[0:8, :], plane[8:16, :]
    tiles = [
        fold(low, lambda q: q, high, lambda q: 7 - q),
        fold(low, lambda q: 4 + q, high, lambda q: 3 - q),
        fold(high, lambda q: q, low, lambda q: 7 - q),
    ]
    return [mirror(at, t) for t in tiles]


def pack_corners(from_ev, from_od, after, msg_od, msg_ev):
    odd_y = is_odd("gy")

    def fill(msg, low, z_low, z_high):
        for at in range(5):
            n = depth(at)
            for k in range(n):
                msg[3 * at + k] = fold_halo(at, z_low, z_high, k if low else 16 - n + k)

    def along_z(odd_z):
        z_low, z_high = (from_ev, from_od) if odd_z else (from_od, from_ev)

        def along_y(odd):
            fill(msg_ev, odd, z_low, z_high)
            fill(msg_od, not odd, z_low, z_high)

        either(odd_y, along_y)

    either(is_odd("gz"), along_z)


W2 = 1.0 / 36.0
GAIN = 1.0 / relax_time
LEFT = 1.0 - GAIN


def gradient(q):
    near, far = 6.0 / 18.0, 6.0 / 36.0
    mid = q[0, 0]
    up_y, down_y, up_z, down_z = q[1, 0], q[-1, 0], q[0, 1], q[0, -1]
    pp, pm, mp, mm = q[1, 1], q[1, -1], q[-1, 1], q[-1, -1]
    along_x = near * mid + far * ((up_y + down_y) + (up_z + down_z))
    diff_y = up_y - down_y
    diff_z = up_z - down_z
    cross = pp - mm
    other = pm - mp
    grad_x = rolled(along_x, -1) - rolled(along_x, 1)
    grad_y = near * diff_y + far * ((cross + other) + (rolled(diff_y, 1) + rolled(diff_y, -1)))
    grad_z = near * diff_z + far * ((cross - other) + (rolled(diff_z, 1) + rolled(diff_z, -1)))
    return grad_x, grad_y, grad_z


def collide(level, rest, tensor, flow, step, share, tail):
    def left(c, post):
        return post if tail is None else post + tail[INDEX[c]]

    def pair(c, even, odd, recolour):
        back = tuple(-v for v in c)
        post = left(c, even + odd)
        yield INDEX[c], post, share * post + recolour
        post = left(back, even - odd)
        yield INDEX[back], post, share * post - recolour

    post = left((0, 0, 0), rest)
    yield 0, post, share * post
    xx, yy, zz, xy, xz, yz = tensor
    diag = (xx, yy, zz)
    lev = [level + d for d in diag]
    for axis in range(3):
        c = tuple(int(a == axis) for a in range(3))
        yield from pair(c, lev[axis] + lev[axis], flow[axis] + flow[axis], step[axis] + step[axis])
    slant = [s * (1.0 / math.sqrt(2.0)) for s in step]
    for a, b, cross in ((0, 1, xy), (0, 2, xz), (1, 2, yz)):
        base = lev[a] + diag[b]
        twice = cross + cross
        c = tuple(int(v in (a, b)) for v in range(3))
        yield from pair(c, base + twice, flow[a] + flow[b], slant[a] + slant[b])
        c = tuple(int(v == a) - int(v == b) for v in range(3))
        yield from pair(c, base - twice, flow[a] - flow[b], slant[a] - slant[b])


def surface(grad):
    square = grad[0] * grad[0] + grad[1] * grad[1] + grad[2] * grad[2]
    root = lax.rsqrt(jnp.maximum(square, 1e-30))
    return square * root, jnp.minimum(root, 1.0 / grad_floor)


def products(vec, other):
    x, y, z = vec
    p, q, r = other
    return [x * p, y * q, z * r, x * q, x * r, y * r]


def step_one(label, dens, vel, grad):
    scale = LEFT * W2
    mix = label * (1.0 - label) * dens
    gmag, inv = surface(grad)
    speed = vel[0] * vel[0] + vel[1] * vel[1] + vel[2] * vel[2]
    scaled = scale * dens

    def relax(pop, eq):
        return pop - (pop - eq) * GAIN

    rest = scaled - 1.5 * scaled * speed
    rest = relax(rest, rest)
    flow = [(3.0 * scaled) * v for v in vel]
    flow = [relax(v, v) for v in flow]
    tensor = products([1.5 * f for f in flow], vel)
    pull = (0.5 * surface_amp * scale) * inv
    tensor = [t + s for t, s in zip(tensor, products([pull * g for g in grad], grad))]
    gm = (0.5 * surface_amp * scale) * gmag
    h = (recolouring_strength * scale) * mix * inv
    return collide(rest - gm, 12.0 * (rest + gm), tensor, flow, [h * g for g in grad], label, None)


def moment(pops, a):
    total = None
    for i, c in enumerate(VELOCITIES):
        if c[a]:
            term = pops[i]
            total = (term if c[a] > 0 else -term) if total is None else (total + term if c[a] > 0 else total - term)
    return total


def step_two(rho, rinv, share, tail, grad):
    mix = share * (1.0 - share) * rho
    gmag, inv = surface(grad)
    scaled = [moment(tail, a) for a in range(3)]
    vel = [(rinv * (1.0 / LEFT)) * m for m in scaled]
    flow = [(3.0 * GAIN * W2 / LEFT) * m for m in scaled]
    tensor = products([1.5 * f for f in flow], vel)
    rest = (GAIN * W2) * rho - (1.0 / 3.0) * (tensor[0] + tensor[1] + tensor[2])
    pull = (0.5 * surface_amp * W2) * inv
    tensor = [t + s for t, s in zip(tensor, products([pull * g for g in grad], grad))]
    gm = (0.5 * surface_amp * W2) * gmag
    h = (recolouring_strength * W2) * mix * inv
    return collide(rest - gm, 12.0 * (rest + gm), tensor, flow, [h * g for g in grad], share, tail)


def streamed_parts(values, weight=None):
    parts = {0: [], 1: [], -1: []}
    for i, c in enumerate(VELOCITIES):
        w = 1 if weight is None else c[weight]
        if w:
            parts[c[0]].append((values[i], w))

    def tree(terms):
        while len(terms) > 1:
            joined = []
            for (a, wa), (b, wb) in zip(terms[::2], terms[1::2]):
                if wa == wb:
                    joined.append((a + b, wa))
                elif wa > 0:
                    joined.append((a - b, 1))
                else:
                    joined.append((b - a, 1))
            terms = joined + terms[len(terms) & ~1 :]
        value, w = terms[0]
        return value if w > 0 else -value

    return {s: tree(terms) if terms else None for s, terms in parts.items()}


def joined(parts):
    side = rolled(parts[1], 1) + rolled(parts[-1], -1)
    return side if parts[0] is None else parts[0] + side


def around(ref, j, k):
    return {(dy, dz): ref[j + dy, 2 + 2 * dz + k : 10 + 2 * dz + k, :] for dy in (-1, 0, 1) for dz in (-1, 0, 1)}


def load_a(refs, j, k):
    return around(refs["label"], j + 1, k), [refs["raw"][at, j + 1, 2 + k : 10 + k, :] for at in range(4)]


def pass_a(refs, j, k, loaded):
    near, (dens, *vel) = loaded
    for i, post, red in step_one(near[0, 0], dens, vel, gradient(near)):
        yield refs["post1"].at[i], j, k, post
        yield refs["red1"].at[i], j, k, red


def incoming(ref, j, k):
    return [ref[i, j - cy, 2 - 2 * cz + k : 10 - 2 * cz + k, :] for i, (_, cy, cz) in enumerate(VELOCITIES)]


def load_b(refs, j, k):
    return incoming(refs["post1"], j + 1, k), incoming(refs["red1"], j + 1, k)


def pass_b(refs, j, k, loaded):
    rho, red = [joined(streamed_parts(v)) * (1.0 / LEFT) for v in loaded]
    rinv = 1.0 / rho
    yield refs["rho_s"], j, k, rho
    yield refs["rinv_s"], j, k, rinv
    yield refs["share_s"], j, k, red * rinv


def load_c(refs, j, k):
    tail = [rolled(v, c[0]) for v, c in zip(incoming(refs["post1"], j + 2, k + 2), VELOCITIES)]
    return tail, around(refs["share_s"], j + 1, k), [refs[name][j + 1, 2 + k : 10 + k, :] for name in ("rho_s", "rinv_s")]


def pass_c(refs, j, k, loaded):
    tail, near, (rho, rinv) = loaded
    for i, post, red in step_two(rho, rinv, near[0, 0], tail, gradient(near)):
        yield refs["post2"].at[i], j, k, post
        yield refs["red2"].at[i], j, k, red


def load_d(refs, j, k):
    return incoming(refs["post2"], j + 1, k), incoming(refs["red2"], j + 1, k)


def pass_d(refs, j, k, loaded):
    post, red = loaded
    parts = streamed_parts(post)
    up, down = rolled(parts[1], 1), rolled(parts[-1], -1)
    rho = parts[0] + (up + down)
    red = joined(streamed_parts(red))
    row = row_index()
    mom_z = joined(streamed_parts(post, 2))
    mom_z = jnp.where(lax.rem(row, 2) == 1, -mom_z, mom_z)
    if k == 0:
        index, at_first, at_last = jnp.where(row < 4, 2 * row, 15 - 2 * row), 0, 12
    else:
        index, at_first, at_last = jnp.where(row < 4, 7 - 2 * row, 2 * row - 8), 8, 4
    for at, v in enumerate([red, rho - red, up - down, joined(streamed_parts(post, 1)), mom_z]):
        v = take_rows(v, index)
        yield refs["edge"].at[at], j, at_first, v[0:4]
        yield refs["edge"].at[at], j, at_last, v[4:8]


PASSES = dict(a=(load_a, pass_a, False), b=(load_b, pass_b, True), c=(load_c, pass_c, False), d=(load_d, pass_d, True))


def sweep(name, refs, rows, tiles, per):
    load, work, defer = PASSES[name]
    count = rows[0][1] - rows[0][0]

    def put(ref, j, k, value):
        ref[j, k : k + value.shape[0], :] = value

    def trip(t, n):
        waiting = []
        for r in range(n):
            for start, _ in rows:
                for k in tiles:
                    j = start + t + r
                    for item in work(refs, j, k, load(refs, j, k)):
                        if defer:
                            waiting.append(item)
                        else:
                            put(*item)
        for item in waiting:
            put(*item)

    if count // per > 1:

        def body(t, carry):
            trip(t * per, per)
            return carry

        lax.fori_loop(0, count // per, body, 0)
    else:
        trip(0, per)
    if count % per:
        trip(count - count % per, count % per)


STATE = dict(
    label=(24, 40, 128),
    raw=(4, 24, 40, 128),
    post1=(19, 22, 32, 128),
    red1=(19, 22, 32, 128),
    rho_s=(20, 32, 128),
    rinv_s=(20, 32, 128),
    share_s=(20, 32, 128),
    post2=(19, 18, 24, 128),
    red2=(19, 18, 24, 128),
    edge=(5, 16, 16, 128),
)
NAMES = list(STATE)


def frame_of(refs, at):
    return refs["label"] if at == 4 else refs["raw"].at[at]


def lay(refs, at, row, plane):
    for t, tile in enumerate(fold_own(at, plane)):
        frame_of(refs, at)[row, 8 + 8 * t : 16 + 8 * t, :] = tile


def middle(when, part, held, phase, density, velocity, *rest):
    refs = dict(zip(NAMES, rest[held + 1 :]))

    def early():
        def body(y, carry):
            for at in range(5):
                lay(refs, at, y + 4, own_plane(at, y, phase, density, velocity))
            return carry

        lax.fori_loop(0, 16, body, 0, unroll=2)
        sweep("a", refs, [(4, 18)], (8, 16, 24), 4)

    def late():
        sweep("b", refs, [(4, 16)], (8, 16), 6)
        sweep("c", refs, [(4, 14)], (8, 16), 5)
        sweep("d", refs, [(4, 12)], (8,), 8)

    pl.when(when())(early)
    if part:
        late()


def first_z():
    return lax.axis_index("gz") == 0


def later_z():
    return lax.axis_index("gz") != 0


def sides(z_ev, z_od, y_od, y_ev, *rest):
    refs = dict(zip(NAMES, rest[len(NAMES) :]))

    def assemble_z(odd):
        low, high = (z_ev, z_od) if odd else (z_od, z_ev)

        def body(y, carry):
            for at in range(5):
                frame_of(refs, at)[y + 4, 0:8, :] = fold_halo(at, low, high, y)
            return carry

        lax.fori_loop(0, 16, body, 0, unroll=4)

    def assemble_y(odd):
        low, high = (y_ev, y_od) if odd else (y_od, y_ev)
        for at in range(5):
            n = depth(at)
            for k in range(n):
                lay(refs, at, 4 - n + k, low[3 * at + k])
                lay(refs, at, 20 + k, high[3 * at + k])

    either(is_odd("gz"), assemble_z)
    either(is_odd("gy"), assemble_y)
    sweep("a", refs, [(0, 4), (18, 22)], (8, 16, 24), 2)
    sweep("a", refs, [(4, 18)], (0,), 7)
    sweep("b", refs, [(0, 4), (16, 20)], (8, 16), 2)
    sweep("b", refs, [(4, 16)], (0,), 12)
    sweep("c", refs, [(0, 4), (14, 18)], (8, 16), 2)
    sweep("c", refs, [(4, 14)], (0,), 10)
    sweep("d", refs, [(0, 4), (12, 16)], (8,), 4)
    sweep("d", refs, [(4, 12)], (0,), 8)


def corners(y_od, y_ev, *rest):
    n = len(NAMES)
    refs = dict(zip(NAMES, rest[n : 2 * n]))
    out_red, out_blue, out_mom, sems = rest[2 * n :]

    def send(start, count, sem):
        outs = [out_red, out_blue, out_mom.at[0], out_mom.at[1], out_mom.at[2]]
        rows = pl.ds(start, count)
        return [pltpu.make_async_copy(refs["edge"].at[f, rows], outs[f].at[rows], sems.at[sem, f]) for f in range(5)]

    first = send(4, 8, 0)
    for c in first:
        c.start()

    def assemble(odd):
        low, high = (y_ev, y_od) if odd else (y_od, y_ev)
        for at in range(5):
            d = depth(at)
            for k in range(d):
                frame_of(refs, at)[4 - d + k, 0:8, :] = low[3 * at + k]
                frame_of(refs, at)[20 + k, 0:8, :] = high[3 * at + k]

    either(is_odd("gy"), assemble)
    sweep("a", refs, [(0, 4), (18, 22)], (0,), 4)
    sweep("b", refs, [(0, 4), (16, 20)], (0,), 4)
    sweep("c", refs, [(0, 4), (14, 18)], (0,), 4)
    sweep("d", refs, [(0, 4), (12, 16)], (0,), 4)
    second = send(0, 4, 1) + send(12, 4, 2)
    for c in second:
        c.start()
    for c in first + second:
        c.wait()


def f32(*shape):
    return jax.ShapeDtypeStruct(shape, jnp.float32)


def swap(value, axis, first):
    count = lax.axis_size(axis)
    pairs = []
    for low in range(first, count, 2):
        high = (low + 1) % count
        pairs += [(low, high), (high, low)]
    return lax.ppermute(value, axis, pairs)


def shards(phase, density, velocity):
    phase, density, velocity = [pltpu.with_memory_space_constraint(v, pltpu.HBM) for v in (phase, density, velocity)]
    in_vmem = pl.BlockSpec(memory_space=pltpu.VMEM)
    in_hbm = pl.BlockSpec(memory_space=pltpu.HBM)
    state = [f32(*s) for s in STATE.values()]
    phase, density, velocity, z_ev, z_od, y_od, y_ev = pl.pallas_call(
        pack_own,
        out_shape=(jax.ShapeDtypeStruct((16, 16, 128), jnp.int32), f32(16, 16, 128), f32(3, 16, 16, 128)) + (f32(16, 16, 128),) * 4,
        in_specs=[in_hbm] * 3,
        out_specs=(in_vmem,) * 7,
        scratch_shapes=[pltpu.SemaphoreType.DMA((3,))],
        compiler_params=vmem(8),
    )(phase, density, velocity)
    n = len(NAMES)

    def do_middle(when, held, token):
        aliases = {3 + i: i for i in range(len(held) + 1)} if held else {3: n}
        *made, token = pl.pallas_call(
            functools.partial(middle, when, bool(held), len(held)),
            out_shape=tuple(state) + (jax.ShapeDtypeStruct(token.shape, token.dtype),),
            in_specs=[in_vmem] * (4 + len(held)),
            out_specs=(in_vmem,) * (n + 1),
            input_output_aliases=aliases,
            compiler_params=vmem(8),
            cost_estimate=pl.CostEstimate(flops=40_000_000, bytes_accessed=20_000_000, transcendentals=0),
        )(phase, density, velocity, *held, token)
        return made, token

    z_ev = swap(z_ev, "gz", 0)
    held, z_od = do_middle(first_z, [], z_od)
    z_od = swap(z_od, "gz", 1)
    y_od = swap(y_od, "gy", 1)
    y_ev = swap(y_ev, "gy", 0)
    held, token = do_middle(later_z, held, jnp.zeros((8, 128), jnp.float32))
    c_od, c_ev = pl.pallas_call(pack_corners, out_shape=(f32(16, 8, 128),) * 2, compiler_params=vmem(4))(z_ev, z_od, token)
    c_od = swap(c_od, "gy", 1)
    c_ev = swap(c_ev, "gy", 0)
    held = pl.pallas_call(
        sides,
        out_shape=tuple(state),
        in_specs=[in_vmem] * (4 + n),
        out_specs=(in_vmem,) * n,
        input_output_aliases={4 + i: i for i in range(n)},
        compiler_params=vmem(8),
        cost_estimate=pl.CostEstimate(flops=10_000_000, bytes_accessed=5_000_000, transcendentals=0),
    )(z_ev, z_od, y_od, y_ev, *held)
    return pl.pallas_call(
        corners,
        out_shape=tuple(state) + (f32(16, 16, 128), f32(16, 16, 128), f32(3, 16, 16, 128)),
        in_specs=[in_vmem] * (2 + n),
        out_specs=(in_vmem,) * n + (in_hbm,) * 3,
        scratch_shapes=[pltpu.SemaphoreType.DMA((3, 5))],
        input_output_aliases={2 + i: i for i in range(n)},
        compiler_params=vmem(8),
    )(c_od, c_ev, *held)[n:]


def solution(mesh):
    placed = (P("gy", "gz", None), P("gy", "gz", None), P(None, "gy", "gz", None))
    return jax.shard_map(
        shards,
        mesh=mesh,
        in_specs=placed,
        out_specs=placed,
        check_vma=False,
    )
```

```python
import functools
import math

import jax
import jax.numpy as jnp
from jax import lax
from jax.experimental import pallas as pl
from jax.experimental.pallas import tpu as pltpu
from jax.sharding import PartitionSpec as P

VELOCITIES = [
    [0, 0, 0],
    [1, 0, 0],
    [-1, 0, 0],
    [0, 1, 0],
    [0, -1, 0],
    [0, 0, 1],
    [0, 0, -1],
    [1, 1, 0],
    [-1, -1, 0],
    [1, -1, 0],
    [-1, 1, 0],
    [1, 0, 1],
    [-1, 0, -1],
    [1, 0, -1],
    [-1, 0, 1],
    [0, 1, 1],
    [0, -1, -1],
    [0, 1, -1],
    [0, -1, 1],
]
INDEX = {tuple(v): i for i, v in enumerate(VELOCITIES)}
relax_time = 0.8
surface_amp = 0.05
recolouring_strength = 0.7
grad_floor = 0.05


def vmem(mib):
    return pltpu.CompilerParams(vmem_limit_bytes=mib * 1024 * 1024)


def rolled(value, shift):
    return pltpu.roll(value, shift % 128, 1) if shift else value


def depth(at):
    return 4 if at == 4 else 3


def fill_z(msg, low, phase, density, velocity):
    for at in range(5):
        n = depth(at)
        start = 0 if low else 16 - n
        if at == 0:
            msg[:, 0:3, :] = density[:, start : start + n, :]
        elif at == 4:
            msg[:, 12:16, :] = phase[:, start : start + n, :].astype(jnp.float32)
        else:
            msg[:, 3 * at : 3 * at + n, :] = velocity[at - 1, :, start : start + n, :]


def fill_y(msg, low, phase, density, velocity):
    for at in range(5):
        for k in range(depth(at)):
            y = k if low else 16 - depth(at) + k
            msg[3 * at + k] = own_plane(at, y, phase, density, velocity)


def own_plane(at, y, phase, density, velocity):
    if at == 0:
        return density[y]
    if at == 4:
        return phase[y].astype(jnp.float32)
    return velocity[at - 1, y]


def is_odd(axis):
    return lax.rem(lax.axis_index(axis), 2) == 1


def either(odd, work):
    @pl.when(odd)
    def _():
        work(True)

    @pl.when(jnp.logical_not(odd))
    def _():
        work(False)


def pack_own(phase_in, density_in, velocity_in, phase, density, velocity, z_ev, z_od, y_od, y_ev, sems):
    copies = [
        pltpu.make_async_copy(velocity_in, velocity, sems.at[0]),
        pltpu.make_async_copy(density_in, density, sems.at[1]),
        pltpu.make_async_copy(phase_in, phase, sems.at[2]),
    ]
    for c in copies:
        c.start()
    for c in copies:
        c.wait()
    own = (phase, density, velocity)

    def along_z(odd):
        fill_z(z_ev, odd, *own)
        fill_z(z_od, not odd, *own)

    def along_y(odd):
        fill_y(y_ev, odd, *own)
        fill_y(y_od, not odd, *own)

    either(is_odd("gz"), along_z)
    either(is_odd("gy"), along_y)


def row_index():
    return lax.broadcasted_iota(jnp.int32, (8, 128), 0)


def take_rows(tile, index):
    return jnp.take_along_axis(tile, index, axis=0)


def fold(low, low_at, high, high_at):
    row = row_index()
    q = lax.shift_right_logical(row, 1)
    odd = lax.rem(row, 2) == 1
    return jnp.where(odd, take_rows(high, high_at(q)), take_rows(low, low_at(q)))


def mirror(at, tile):
    return jnp.where(lax.rem(row_index(), 2) == 1, -tile, tile) if at == 3 else tile


def fold_halo(at, low, high, y):
    start, off = (8, 4) if at == 4 else (8, 1) if at == 3 else (3 * at, 0)
    n = depth(at)
    low, high = low[y, start : start + 8, :], high[y, start : start + 8, :]
    return mirror(at, fold(low, lambda q: off + jnp.maximum(q - (4 - n), 0), high, lambda q: off + jnp.minimum(3 - q, n - 1)))


def fold_own(at, plane):
    low, high = plane[0:8, :], plane[8:16, :]
    tiles = [
        fold(low, lambda q: q, high, lambda q: 7 - q),
        fold(low, lambda q: 4 + q, high, lambda q: 3 - q),
        fold(high, lambda q: q, low, lambda q: 7 - q),
    ]
    return [mirror(at, t) for t in tiles]


def pack_corners(from_ev, from_od, after, msg_od, msg_ev):
    odd_y = is_odd("gy")

    def fill(msg, low, z_low, z_high):
        for at in range(5):
            n = depth(at)
            for k in range(n):
                msg[3 * at + k] = fold_halo(at, z_low, z_high, k if low else 16 - n + k)

    def along_z(odd_z):
        z_low, z_high = (from_ev, from_od) if odd_z else (from_od, from_ev)

        def along_y(odd):
            fill(msg_ev, odd, z_low, z_high)
            fill(msg_od, not odd, z_low, z_high)

        either(odd_y, along_y)

    either(is_odd("gz"), along_z)


W2 = 1.0 / 36.0
GAIN = 1.0 / relax_time
LEFT = 1.0 - GAIN


def gradient(q):
    near, far = 6.0 / 18.0, 6.0 / 36.0
    mid = q[0, 0]
    up_y, down_y, up_z, down_z = q[1, 0], q[-1, 0], q[0, 1], q[0, -1]
    pp, pm, mp, mm = q[1, 1], q[1, -1], q[-1, 1], q[-1, -1]
    along_x = near * mid + far * ((up_y + down_y) + (up_z + down_z))
    diff_y = up_y - down_y
    diff_z = up_z - down_z
    cross = pp - mm
    other = pm - mp
    grad_x = rolled(along_x, -1) - rolled(along_x, 1)
    grad_y = near * diff_y + far * ((cross + other) + (rolled(diff_y, 1) + rolled(diff_y, -1)))
    grad_z = near * diff_z + far * ((cross - other) + (rolled(diff_z, 1) + rolled(diff_z, -1)))
    return grad_x, grad_y, grad_z


def collide(level, rest, tensor, flow, step, share, tail):
    def left(c, post):
        return post if tail is None else post + tail[INDEX[c]]

    def pair(c, even, odd, recolour):
        back = tuple(-v for v in c)
        post = left(c, even + odd)
        yield INDEX[c], post, share * post + recolour
        post = left(back, even - odd)
        yield INDEX[back], post, share * post - recolour

    post = left((0, 0, 0), rest)
    yield 0, post, share * post
    xx, yy, zz, xy, xz, yz = tensor
    diag = (xx, yy, zz)
    lev = [level + d for d in diag]
    for axis in range(3):
        c = tuple(int(a == axis) for a in range(3))
        yield from pair(c, lev[axis] + lev[axis], flow[axis] + flow[axis], step[axis] + step[axis])
    slant = [s * (1.0 / math.sqrt(2.0)) for s in step]
    for a, b, cross in ((0, 1, xy), (0, 2, xz), (1, 2, yz)):
        base = lev[a] + diag[b]
        twice = cross + cross
        c = tuple(int(v in (a, b)) for v in range(3))
        yield from pair(c, base + twice, flow[a] + flow[b], slant[a] + slant[b])
        c = tuple(int(v == a) - int(v == b) for v in range(3))
        yield from pair(c, base - twice, flow[a] - flow[b], slant[a] - slant[b])


def surface(grad):
    square = grad[0] * grad[0] + grad[1] * grad[1] + grad[2] * grad[2]
    root = lax.rsqrt(jnp.maximum(square, 1e-30))
    return square * root, jnp.minimum(root, 1.0 / grad_floor)


def products(vec, other):
    x, y, z = vec
    p, q, r = other
    return [x * p, y * q, z * r, x * q, x * r, y * r]


def step_one(label, dens, vel, grad):
    scale = LEFT * W2
    mix = label * (1.0 - label) * dens
    gmag, inv = surface(grad)
    speed = vel[0] * vel[0] + vel[1] * vel[1] + vel[2] * vel[2]
    scaled = scale * dens

    def relax(pop, eq):
        return pop - (pop - eq) * GAIN

    rest = scaled - 1.5 * scaled * speed
    rest = relax(rest, rest)
    flow = [(3.0 * scaled) * v for v in vel]
    flow = [relax(v, v) for v in flow]
    tensor = products([1.5 * f for f in flow], vel)
    pull = (0.5 * surface_amp * scale) * inv
    tensor = [t + s for t, s in zip(tensor, products([pull * g for g in grad], grad))]
    gm = (0.5 * surface_amp * scale) * gmag
    h = (recolouring_strength * scale) * mix * inv
    return collide(rest - gm, 12.0 * (rest + gm), tensor, flow, [h * g for g in grad], label, None)


def moment(pops, a):
    total = None
    for i, c in enumerate(VELOCITIES):
        if c[a]:
            term = pops[i]
            total = (term if c[a] > 0 else -term) if total is None else (total + term if c[a] > 0 else total - term)
    return total


def step_two(rho, rinv, share, tail, grad):
    mix = share * (1.0 - share) * rho
    gmag, inv = surface(grad)
    scaled = [moment(tail, a) for a in range(3)]
    vel = [(rinv * (1.0 / LEFT)) * m for m in scaled]
    flow = [(3.0 * GAIN * W2 / LEFT) * m for m in scaled]
    tensor = products([1.5 * f for f in flow], vel)
    rest = (GAIN * W2) * rho - (1.0 / 3.0) * (tensor[0] + tensor[1] + tensor[2])
    pull = (0.5 * surface_amp * W2) * inv
    tensor = [t + s for t, s in zip(tensor, products([pull * g for g in grad], grad))]
    gm = (0.5 * surface_amp * W2) * gmag
    h = (recolouring_strength * W2) * mix * inv
    return collide(rest - gm, 12.0 * (rest + gm), tensor, flow, [h * g for g in grad], share, tail)


def streamed_parts(values, weight=None):
    parts = {0: [], 1: [], -1: []}
    for i, c in enumerate(VELOCITIES):
        w = 1 if weight is None else c[weight]
        if w:
            parts[c[0]].append((values[i], w))

    def tree(terms):
        while len(terms) > 1:
            joined = []
            for (a, wa), (b, wb) in zip(terms[::2], terms[1::2]):
                if wa == wb:
                    joined.append((a + b, wa))
                elif wa > 0:
                    joined.append((a - b, 1))
                else:
                    joined.append((b - a, 1))
            terms = joined + terms[len(terms) & ~1 :]
        value, w = terms[0]
        return value if w > 0 else -value

    return {s: tree(terms) if terms else None for s, terms in parts.items()}


def joined(parts):
    side = rolled(parts[1], 1) + rolled(parts[-1], -1)
    return side if parts[0] is None else parts[0] + side


def around(ref, j, k):
    return {(dy, dz): ref[j + dy, 2 + 2 * dz + k : 10 + 2 * dz + k, :] for dy in (-1, 0, 1) for dz in (-1, 0, 1)}


def load_a(refs, j, k):
    return around(refs["label"], j + 1, k), [refs["raw"][at, j + 1, 2 + k : 10 + k, :] for at in range(4)]


def pass_a(refs, j, k, loaded):
    near, (dens, *vel) = loaded
    for i, post, red in step_one(near[0, 0], dens, vel, gradient(near)):
        yield refs["post1"].at[i], j, k, post
        yield refs["red1"].at[i], j, k, red


def incoming(ref, j, k):
    return [ref[i, j - cy, 2 - 2 * cz + k : 10 - 2 * cz + k, :] for i, (_, cy, cz) in enumerate(VELOCITIES)]


def load_b(refs, j, k):
    return incoming(refs["post1"], j + 1, k), incoming(refs["red1"], j + 1, k)


def pass_b(refs, j, k, loaded):
    rho, red = [joined(streamed_parts(v)) * (1.0 / LEFT) for v in loaded]
    rinv = 1.0 / rho
    yield refs["rho_s"], j, k, rho
    yield refs["rinv_s"], j, k, rinv
    yield refs["share_s"], j, k, red * rinv


def load_c(refs, j, k):
    tail = [rolled(v, c[0]) for v, c in zip(incoming(refs["post1"], j + 2, k + 2), VELOCITIES)]
    return tail, around(refs["share_s"], j + 1, k), [refs[name][j + 1, 2 + k : 10 + k, :] for name in ("rho_s", "rinv_s")]


def pass_c(refs, j, k, loaded):
    tail, near, (rho, rinv) = loaded
    for i, post, red in step_two(rho, rinv, near[0, 0], tail, gradient(near)):
        yield refs["post2"].at[i], j, k, post
        yield refs["red2"].at[i], j, k, red


def load_d(refs, j, k):
    return incoming(refs["post2"], j + 1, k), incoming(refs["red2"], j + 1, k)


def pass_d(refs, j, k, loaded):
    post, red = loaded
    parts = streamed_parts(post)
    up, down = rolled(parts[1], 1), rolled(parts[-1], -1)
    rho = parts[0] + (up + down)
    red = joined(streamed_parts(red))
    row = row_index()
    mom_z = joined(streamed_parts(post, 2))
    mom_z = jnp.where(lax.rem(row, 2) == 1, -mom_z, mom_z)
    if k == 0:
        index, at_first, at_last = jnp.where(row < 4, 2 * row, 15 - 2 * row), 0, 12
    else:
        index, at_first, at_last = jnp.where(row < 4, 7 - 2 * row, 2 * row - 8), 8, 4
    for at, v in enumerate([red, rho - red, up - down, joined(streamed_parts(post, 1)), mom_z]):
        v = take_rows(v, index)
        yield refs["edge"].at[at], j, at_first, v[0:4]
        yield refs["edge"].at[at], j, at_last, v[4:8]


PASSES = dict(a=(load_a, pass_a, False), b=(load_b, pass_b, True), c=(load_c, pass_c, False), d=(load_d, pass_d, True))


def sweep(name, refs, rows, tiles, per):
    load, work, defer = PASSES[name]
    count = rows[0][1] - rows[0][0]

    def put(ref, j, k, value):
        ref[j, k : k + value.shape[0], :] = value

    def trip(t, n):
        waiting = []
        for r in range(n):
            for start, _ in rows:
                for k in tiles:
                    j = start + t + r
                    for item in work(refs, j, k, load(refs, j, k)):
                        if defer:
                            waiting.append(item)
                        else:
                            put(*item)
        for item in waiting:
            put(*item)

    if count // per > 1:

        def body(t, carry):
            trip(t * per, per)
            return carry

        lax.fori_loop(0, count // per, body, 0)
    else:
        trip(0, per)
    if count % per:
        trip(count - count % per, count % per)


STATE = dict(
    label=(24, 40, 128),
    raw=(4, 24, 40, 128),
    post1=(19, 22, 32, 128),
    red1=(19, 22, 32, 128),
    rho_s=(20, 32, 128),
    rinv_s=(20, 32, 128),
    share_s=(20, 32, 128),
    post2=(19, 18, 24, 128),
    red2=(19, 18, 24, 128),
    edge=(5, 16, 16, 128),
)
NAMES = list(STATE)


def frame_of(refs, at):
    return refs["label"] if at == 4 else refs["raw"].at[at]


def lay(refs, at, row, plane):
    for t, tile in enumerate(fold_own(at, plane)):
        frame_of(refs, at)[row, 8 + 8 * t : 16 + 8 * t, :] = tile


def middle(jobs, held, passed, phase, density, velocity, *rest):
    refs = dict(zip(NAMES, rest[held + passed :]))

    def lay_own():
        def body(y, carry):
            for at in range(5):
                lay(refs, at, y + 4, own_plane(at, y, phase, density, velocity))
            return carry

        lax.fori_loop(0, 16, body, 0, unroll=2)

    parts = dict(
        l=lay_own,
        a=lambda: sweep("a", refs, [(4, 18)], (8, 16, 24), 14),
        b=lambda: sweep("b", refs, [(4, 16)], (8, 16), 12),
        c=lambda: sweep("c", refs, [(4, 14)], (8, 16), 5),
        d=lambda: sweep("d", refs, [(4, 12)], (8,), 8),
    )
    for when, names in jobs:

        def work(names=names):
            for name in names:
                parts[name]()

        if when is None:
            work()
        else:
            pl.when(when())(work)


FIRST, SECOND, LAST = "la", "bcd", ""


def first_z():
    return lax.axis_index("gz") == 0


def later_z():
    return lax.axis_index("gz") != 0


def sides(z_ev, z_od, y_od, y_ev, *rest):
    refs = dict(zip(NAMES, rest[len(NAMES) :]))

    def assemble_z(odd):
        low, high = (z_ev, z_od) if odd else (z_od, z_ev)

        def body(y, carry):
            for at in range(5):
                frame_of(refs, at)[y + 4, 0:8, :] = fold_halo(at, low, high, y)
            return carry

        lax.fori_loop(0, 16, body, 0, unroll=4)

    def assemble_y(odd):
        low, high = (y_ev, y_od) if odd else (y_od, y_ev)
        for at in range(5):
            n = depth(at)
            for k in range(n):
                lay(refs, at, 4 - n + k, low[3 * at + k])
                lay(refs, at, 20 + k, high[3 * at + k])

    either(is_odd("gz"), assemble_z)
    either(is_odd("gy"), assemble_y)
    sweep("a", refs, [(0, 4), (18, 22)], (8, 16, 24), 4)
    sweep("a", refs, [(4, 18)], (0,), 14)
    sweep("b", refs, [(0, 4), (16, 20)], (8, 16), 4)
    sweep("b", refs, [(4, 16)], (0,), 12)
    sweep("c", refs, [(0, 4), (14, 18)], (8, 16), 4)
    sweep("c", refs, [(4, 14)], (0,), 10)
    sweep("d", refs, [(0, 4), (12, 16)], (8,), 4)
    sweep("d", refs, [(4, 12)], (0,), 8)


def corners(y_od, y_ev, *rest):
    n = len(NAMES)
    refs = dict(zip(NAMES, rest[n : 2 * n]))
    out_red, out_blue, out_mom, sems = rest[2 * n :]

    def send(start, count, sem):
        rows, edge = pl.ds(start, count), refs["edge"]
        pairs = [(edge.at[0, rows], out_red.at[rows]), (edge.at[1, rows], out_blue.at[rows]), (edge.at[2:5, rows], out_mom.at[:, rows])]
        return [pltpu.make_async_copy(src, dst, sems.at[sem, f]) for f, (src, dst) in enumerate(pairs)]

    first = send(4, 8, 0)
    for c in first:
        c.start()

    def assemble(odd):
        low, high = (y_ev, y_od) if odd else (y_od, y_ev)
        for at in range(5):
            d = depth(at)
            for k in range(d):
                frame_of(refs, at)[4 - d + k, 0:8, :] = low[3 * at + k]
                frame_of(refs, at)[20 + k, 0:8, :] = high[3 * at + k]

    either(is_odd("gy"), assemble)
    sweep("a", refs, [(0, 4), (18, 22)], (0,), 4)
    sweep("b", refs, [(0, 4), (16, 20)], (0,), 4)
    sweep("c", refs, [(0, 4), (14, 18)], (0,), 4)
    sweep("d", refs, [(0, 4), (12, 16)], (0,), 4)
    second = send(0, 4, 1) + send(12, 4, 2)
    for c in second:
        c.start()
    for c in first + second:
        c.wait()


def f32(*shape):
    return jax.ShapeDtypeStruct(shape, jnp.float32)


def swap(value, axis, first):
    count = lax.axis_size(axis)
    pairs = []
    for low in range(first, count, 2):
        high = (low + 1) % count
        pairs += [(low, high), (high, low)]
    return lax.ppermute(value, axis, pairs)


def shards(phase, density, velocity):
    phase, density, velocity = [pltpu.with_memory_space_constraint(v, pltpu.HBM) for v in (phase, density, velocity)]
    in_vmem = pl.BlockSpec(memory_space=pltpu.VMEM)
    in_hbm = pl.BlockSpec(memory_space=pltpu.HBM)
    state = [f32(*s) for s in STATE.values()]
    phase, density, velocity, z_ev, z_od, y_od, y_ev = pl.pallas_call(
        pack_own,
        out_shape=(jax.ShapeDtypeStruct((16, 16, 128), jnp.int32), f32(16, 16, 128), f32(3, 16, 16, 128)) + (f32(16, 16, 128),) * 4,
        in_specs=[in_hbm] * 3,
        out_specs=(in_vmem,) * 7,
        scratch_shapes=[pltpu.SemaphoreType.DMA((3,))],
        compiler_params=vmem(8),
    )(phase, density, velocity)
    n = len(NAMES)

    def do_middle(jobs, held, *tokens):
        h, p = len(held), len(tokens)
        made = pl.pallas_call(
            functools.partial(middle, jobs, h, p),
            out_shape=tuple(state) + tuple(jax.ShapeDtypeStruct(t.shape, t.dtype) for t in tokens),
            in_specs=[in_vmem] * (3 + h + p),
            out_specs=(in_vmem,) * (n + p),
            input_output_aliases={3 + i: i + n - h for i in range(h + p)},
            compiler_params=vmem(8),
            cost_estimate=pl.CostEstimate(flops=40_000_000, bytes_accessed=20_000_000, transcendentals=0),
        )(phase, density, velocity, *held, *tokens)
        return made[:n], *made[n:]

    held = []
    if FIRST:
        held, z_ev, z_od = do_middle([(first_z, FIRST)], held, z_ev, z_od)
    z_ev = swap(z_ev, "gz", 0)
    if SECOND:
        held, z_od = do_middle([(first_z, SECOND)], held, z_od)
    z_od = swap(z_od, "gz", 1)
    y_od = swap(y_od, "gy", 1)
    y_ev = swap(y_ev, "gy", 0)
    early = FIRST + SECOND
    jobs = [(later_z, early)] + ([(None, LAST)] if LAST else [])
    held, token = do_middle(jobs, held, jnp.zeros((8, 128), jnp.float32))
    c_od, c_ev = pl.pallas_call(pack_corners, out_shape=(f32(16, 8, 128),) * 2, compiler_params=vmem(4))(z_ev, z_od, token)
    c_od = swap(c_od, "gy", 1)
    c_ev = swap(c_ev, "gy", 0)
    held = pl.pallas_call(
        sides,
        out_shape=tuple(state),
        in_specs=[in_vmem] * (4 + n),
        out_specs=(in_vmem,) * n,
        input_output_aliases={4 + i: i for i in range(n)},
        compiler_params=vmem(8),
        cost_estimate=pl.CostEstimate(flops=10_000_000, bytes_accessed=5_000_000, transcendentals=0),
    )(z_ev, z_od, y_od, y_ev, *held)
    return pl.pallas_call(
        corners,
        out_shape=tuple(state) + (f32(16, 16, 128), f32(16, 16, 128), f32(3, 16, 16, 128)),
        in_specs=[in_vmem] * (2 + n),
        out_specs=(in_vmem,) * n + (in_hbm,) * 3,
        scratch_shapes=[pltpu.SemaphoreType.DMA((3, 3))],
        input_output_aliases={2 + i: i for i in range(n)},
        compiler_params=vmem(8),
    )(c_od, c_ev, *held)[n:]


def solution(mesh):
    placed = (P("gy", "gz", None), P("gy", "gz", None), P(None, "gy", "gz", None))
    return jax.shard_map(
        shards,
        mesh=mesh,
        in_specs=placed,
        out_specs=placed,
        check_vma=False,
    )
```

```python
import functools
import math

import jax
import jax.numpy as jnp
from jax import lax
from jax.experimental import pallas as pl
from jax.experimental.pallas import tpu as pltpu
from jax.sharding import PartitionSpec as P

VELOCITIES = [
    [0, 0, 0],
    [1, 0, 0],
    [-1, 0, 0],
    [0, 1, 0],
    [0, -1, 0],
    [0, 0, 1],
    [0, 0, -1],
    [1, 1, 0],
    [-1, -1, 0],
    [1, -1, 0],
    [-1, 1, 0],
    [1, 0, 1],
    [-1, 0, -1],
    [1, 0, -1],
    [-1, 0, 1],
    [0, 1, 1],
    [0, -1, -1],
    [0, 1, -1],
    [0, -1, 1],
]
INDEX = {tuple(v): i for i, v in enumerate(VELOCITIES)}
relax_time = 0.8
surface_amp = 0.05
recolouring_strength = 0.7
grad_floor = 0.05


def vmem(mib):
    return pltpu.CompilerParams(vmem_limit_bytes=mib * 1024 * 1024)


def rolled(value, shift):
    return pltpu.roll(value, shift % 128, 1) if shift else value


def depth(at):
    return 4 if at == 4 else 3


def fill_z(msg, low, phase, density, velocity):
    for at in range(5):
        n = depth(at)
        start = 0 if low else 16 - n
        if at == 0:
            msg[:, 0:3, :] = density[:, start : start + n, :]
        elif at == 4:
            msg[:, 12:16, :] = phase[:, start : start + n, :].astype(jnp.float32)
        else:
            msg[:, 3 * at : 3 * at + n, :] = velocity[at - 1, :, start : start + n, :]


def fill_y(msg, low, phase, density, velocity):
    for at in range(5):
        for k in range(depth(at)):
            y = k if low else 16 - depth(at) + k
            msg[3 * at + k] = own_plane(at, y, phase, density, velocity)


def own_plane(at, y, phase, density, velocity):
    if at == 0:
        return density[y]
    if at == 4:
        return phase[y].astype(jnp.float32)
    return velocity[at - 1, y]


def is_odd(axis):
    return lax.rem(lax.axis_index(axis), 2) == 1


def either(odd, work):
    @pl.when(odd)
    def _():
        work(True)

    @pl.when(jnp.logical_not(odd))
    def _():
        work(False)


def pack_own(phase_in, density_in, velocity_in, phase, density, velocity, z_ev, z_od, y_od, y_ev, sems):
    copies = [
        pltpu.make_async_copy(velocity_in, velocity, sems.at[0]),
        pltpu.make_async_copy(density_in, density, sems.at[1]),
        pltpu.make_async_copy(phase_in, phase, sems.at[2]),
    ]
    for c in copies:
        c.start()
    for c in copies:
        c.wait()
    own = (phase, density, velocity)

    def along_z(odd):
        fill_z(z_ev, odd, *own)
        fill_z(z_od, not odd, *own)

    def along_y(odd):
        fill_y(y_ev, odd, *own)
        fill_y(y_od, not odd, *own)

    either(is_odd("gz"), along_z)
    either(is_odd("gy"), along_y)


def row_index():
    return lax.broadcasted_iota(jnp.int32, (8, 128), 0)


def take_rows(tile, index):
    return jnp.take_along_axis(tile, index, axis=0)


def fold(low, low_at, high, high_at):
    row = row_index()
    q = lax.shift_right_logical(row, 1)
    odd = lax.rem(row, 2) == 1
    return jnp.where(odd, take_rows(high, high_at(q)), take_rows(low, low_at(q)))


def mirror(at, tile):
    return jnp.where(lax.rem(row_index(), 2) == 1, -tile, tile) if at == 3 else tile


def fold_halo(at, low, high, y):
    start, off = (8, 4) if at == 4 else (8, 1) if at == 3 else (3 * at, 0)
    n = depth(at)
    low, high = low[y, start : start + 8, :], high[y, start : start + 8, :]
    return mirror(at, fold(low, lambda q: off + jnp.maximum(q - (4 - n), 0), high, lambda q: off + jnp.minimum(3 - q, n - 1)))


def fold_own(at, plane):
    low, high = plane[0:8, :], plane[8:16, :]
    tiles = [
        fold(low, lambda q: q, high, lambda q: 7 - q),
        fold(low, lambda q: 4 + q, high, lambda q: 3 - q),
        fold(high, lambda q: q, low, lambda q: 7 - q),
    ]
    return [mirror(at, t) for t in tiles]


def pack_corners(from_ev, from_od, after, msg_od, msg_ev):
    odd_y = is_odd("gy")

    def fill(msg, low, z_low, z_high):
        for at in range(5):
            n = depth(at)
            for k in range(n):
                msg[3 * at + k] = fold_halo(at, z_low, z_high, k if low else 16 - n + k)

    def along_z(odd_z):
        z_low, z_high = (from_ev, from_od) if odd_z else (from_od, from_ev)

        def along_y(odd):
            fill(msg_ev, odd, z_low, z_high)
            fill(msg_od, not odd, z_low, z_high)

        either(odd_y, along_y)

    either(is_odd("gz"), along_z)


W2 = 1.0 / 36.0
GAIN = 1.0 / relax_time
LEFT = 1.0 - GAIN


def gradient(q):
    near, far = 6.0 / 18.0, 6.0 / 36.0
    mid = q[0, 0]
    up_y, down_y, up_z, down_z = q[1, 0], q[-1, 0], q[0, 1], q[0, -1]
    pp, pm, mp, mm = q[1, 1], q[1, -1], q[-1, 1], q[-1, -1]
    along_x = near * mid + far * ((up_y + down_y) + (up_z + down_z))
    diff_y = up_y - down_y
    diff_z = up_z - down_z
    cross = pp - mm
    other = pm - mp
    grad_x = rolled(along_x, -1) - rolled(along_x, 1)
    grad_y = near * diff_y + far * ((cross + other) + (rolled(diff_y, 1) + rolled(diff_y, -1)))
    grad_z = near * diff_z + far * ((cross - other) + (rolled(diff_z, 1) + rolled(diff_z, -1)))
    return grad_x, grad_y, grad_z


def collide(level, rest, tensor, flow, step, share, tail):
    def left(c, post):
        return post if tail is None else post + tail[INDEX[c]]

    def pair(c, even, odd, recolour):
        back = tuple(-v for v in c)
        post = left(c, even + odd)
        yield INDEX[c], post, share * post + recolour
        post = left(back, even - odd)
        yield INDEX[back], post, share * post - recolour

    post = left((0, 0, 0), rest)
    yield 0, post, share * post
    xx, yy, zz, xy, xz, yz = tensor
    diag = (xx, yy, zz)
    lev = [level + d for d in diag]
    for axis in range(3):
        c = tuple(int(a == axis) for a in range(3))
        yield from pair(c, lev[axis] + lev[axis], flow[axis] + flow[axis], step[axis] + step[axis])
    slant = [s * (1.0 / math.sqrt(2.0)) for s in step]
    for a, b, cross in ((0, 1, xy), (0, 2, xz), (1, 2, yz)):
        base = lev[a] + diag[b]
        twice = cross + cross
        c = tuple(int(v in (a, b)) for v in range(3))
        yield from pair(c, base + twice, flow[a] + flow[b], slant[a] + slant[b])
        c = tuple(int(v == a) - int(v == b) for v in range(3))
        yield from pair(c, base - twice, flow[a] - flow[b], slant[a] - slant[b])


def surface(grad):
    square = grad[0] * grad[0] + grad[1] * grad[1] + grad[2] * grad[2]
    root = lax.rsqrt(jnp.maximum(square, 1e-30))
    return square * root, jnp.minimum(root, 1.0 / grad_floor)


def products(vec, other):
    x, y, z = vec
    p, q, r = other
    return [x * p, y * q, z * r, x * q, x * r, y * r]


def step_one(label, dens, vel, grad):
    scale = LEFT * W2
    mix = label * (1.0 - label) * dens
    gmag, inv = surface(grad)
    speed = vel[0] * vel[0] + vel[1] * vel[1] + vel[2] * vel[2]
    scaled = scale * dens

    def relax(pop, eq):
        return pop - (pop - eq) * GAIN

    rest = scaled - 1.5 * scaled * speed
    rest = relax(rest, rest)
    flow = [(3.0 * scaled) * v for v in vel]
    flow = [relax(v, v) for v in flow]
    tensor = products([1.5 * f for f in flow], vel)
    pull = (0.5 * surface_amp * scale) * inv
    tensor = [t + s for t, s in zip(tensor, products([pull * g for g in grad], grad))]
    gm = (0.5 * surface_amp * scale) * gmag
    h = (recolouring_strength * scale) * mix * inv
    return collide(rest - gm, 12.0 * (rest + gm), tensor, flow, [h * g for g in grad], label, None)


def moment(pops, a):
    total = None
    for i, c in enumerate(VELOCITIES):
        if c[a]:
            term = pops[i]
            total = (term if c[a] > 0 else -term) if total is None else (total + term if c[a] > 0 else total - term)
    return total


def step_two(rho, rinv, share, tail, grad):
    mix = share * (1.0 - share) * rho
    gmag, inv = surface(grad)
    scaled = [moment(tail, a) for a in range(3)]
    vel = [(rinv * (1.0 / LEFT)) * m for m in scaled]
    flow = [(3.0 * GAIN * W2 / LEFT) * m for m in scaled]
    tensor = products([1.5 * f for f in flow], vel)
    rest = (GAIN * W2) * rho - (1.0 / 3.0) * (tensor[0] + tensor[1] + tensor[2])
    pull = (0.5 * surface_amp * W2) * inv
    tensor = [t + s for t, s in zip(tensor, products([pull * g for g in grad], grad))]
    gm = (0.5 * surface_amp * W2) * gmag
    h = (recolouring_strength * W2) * mix * inv
    return collide(rest - gm, 12.0 * (rest + gm), tensor, flow, [h * g for g in grad], share, tail)


def streamed_parts(values, weight=None):
    parts = {0: [], 1: [], -1: []}
    for i, c in enumerate(VELOCITIES):
        w = 1 if weight is None else c[weight]
        if w:
            parts[c[0]].append((values[i], w))

    def tree(terms):
        while len(terms) > 1:
            joined = []
            for (a, wa), (b, wb) in zip(terms[::2], terms[1::2]):
                if wa == wb:
                    joined.append((a + b, wa))
                elif wa > 0:
                    joined.append((a - b, 1))
                else:
                    joined.append((b - a, 1))
            terms = joined + terms[len(terms) & ~1 :]
        value, w = terms[0]
        return value if w > 0 else -value

    return {s: tree(terms) if terms else None for s, terms in parts.items()}


def joined(parts):
    side = rolled(parts[1], 1) + rolled(parts[-1], -1)
    return side if parts[0] is None else parts[0] + side


def around(ref, j, k):
    return {(dy, dz): ref[j + dy, 2 + 2 * dz + k : 10 + 2 * dz + k, :] for dy in (-1, 0, 1) for dz in (-1, 0, 1)}


def load_a(refs, j, k):
    return around(refs["label"], j + 1, k), [refs["raw"][at, j + 1, 2 + k : 10 + k, :] for at in range(4)]


def pass_a(refs, j, k, loaded):
    near, (dens, *vel) = loaded
    for i, post, red in step_one(near[0, 0], dens, vel, gradient(near)):
        yield refs["post1"].at[i], j, k, post
        yield refs["red1"].at[i], j, k, red


def incoming(ref, j, k):
    return [ref[i, j - cy, 2 - 2 * cz + k : 10 - 2 * cz + k, :] for i, (_, cy, cz) in enumerate(VELOCITIES)]


def load_b(refs, j, k):
    return incoming(refs["post1"], j + 1, k), incoming(refs["red1"], j + 1, k)


def pass_b(refs, j, k, loaded):
    rho, red = [joined(streamed_parts(v)) * (1.0 / LEFT) for v in loaded]
    rinv = 1.0 / rho
    yield refs["rho_s"], j, k, rho
    yield refs["rinv_s"], j, k, rinv
    yield refs["share_s"], j, k, red * rinv


def load_c(refs, j, k):
    tail = [rolled(v, c[0]) for v, c in zip(incoming(refs["post1"], j + 2, k + 2), VELOCITIES)]
    return tail, around(refs["share_s"], j + 1, k), [refs[name][j + 1, 2 + k : 10 + k, :] for name in ("rho_s", "rinv_s")]


def pass_c(refs, j, k, loaded):
    tail, near, (rho, rinv) = loaded
    for i, post, red in step_two(rho, rinv, near[0, 0], tail, gradient(near)):
        yield refs["post2"].at[i], j, k, post
        yield refs["red2"].at[i], j, k, red


def load_d(refs, j, k):
    return incoming(refs["post2"], j + 1, k), incoming(refs["red2"], j + 1, k)


def pass_d(refs, j, k, loaded):
    post, red = loaded
    parts = streamed_parts(post)
    up, down = rolled(parts[1], 1), rolled(parts[-1], -1)
    rho = parts[0] + (up + down)
    red = joined(streamed_parts(red))
    row = row_index()
    mom_z = joined(streamed_parts(post, 2))
    mom_z = jnp.where(lax.rem(row, 2) == 1, -mom_z, mom_z)
    if k == 0:
        index, at_first, at_last = jnp.where(row < 4, 2 * row, 15 - 2 * row), 0, 12
    else:
        index, at_first, at_last = jnp.where(row < 4, 7 - 2 * row, 2 * row - 8), 8, 4
    for at, v in enumerate([red, rho - red, up - down, joined(streamed_parts(post, 1)), mom_z]):
        v = take_rows(v, index)
        yield refs["edge"].at[at], j, at_first, v[0:4]
        yield refs["edge"].at[at], j, at_last, v[4:8]


PASSES = dict(a=(load_a, pass_a, False), b=(load_b, pass_b, True), c=(load_c, pass_c, False), d=(load_d, pass_d, True))


def sweep(name, refs, rows, tiles, per):
    load, work, defer = PASSES[name]
    count = rows[0][1] - rows[0][0]

    def put(ref, j, k, value):
        ref[j, k : k + value.shape[0], :] = value

    def trip(t, n):
        waiting = []
        for r in range(n):
            for start, _ in rows:
                for k in tiles:
                    j = start + t + r
                    for item in work(refs, j, k, load(refs, j, k)):
                        if defer:
                            waiting.append(item)
                        else:
                            put(*item)
        for item in waiting:
            put(*item)

    if count // per > 1:

        def body(t, carry):
            trip(t * per, per)
            return carry

        lax.fori_loop(0, count // per, body, 0)
    else:
        trip(0, per)
    if count % per:
        trip(count - count % per, count % per)


STATE = dict(
    label=(24, 40, 128),
    raw=(4, 24, 40, 128),
    post1=(19, 22, 32, 128),
    red1=(19, 22, 32, 128),
    rho_s=(20, 32, 128),
    rinv_s=(20, 32, 128),
    share_s=(20, 32, 128),
    post2=(19, 18, 24, 128),
    red2=(19, 18, 24, 128),
    edge=(5, 16, 16, 128),
)
NAMES = list(STATE)


def frame_of(refs, at):
    return refs["label"] if at == 4 else refs["raw"].at[at]


def lay(refs, at, row, plane):
    for t, tile in enumerate(fold_own(at, plane)):
        frame_of(refs, at)[row, 8 + 8 * t : 16 + 8 * t, :] = tile


def middle(jobs, held, passed, phase, density, velocity, *rest):
    refs = dict(zip(NAMES, rest[held + passed :]))

    def lay_own():
        def body(y, carry):
            for at in range(5):
                lay(refs, at, y + 4, own_plane(at, y, phase, density, velocity))
            return carry

        lax.fori_loop(0, 16, body, 0, unroll=4)

    parts = dict(
        l=lay_own,
        a=lambda: sweep("a", refs, [(4, 18)], (8, 16, 24), 14),
        b=lambda: sweep("b", refs, [(4, 16)], (8, 16), 12),
        c=lambda: sweep("c", refs, [(4, 14)], (8, 16), 5),
        d=lambda: sweep("d", refs, [(4, 12)], (8,), 8),
    )
    for when, names in jobs:

        def work(names=names):
            for name in names:
                parts[name]()

        if when is None:
            work()
        else:
            pl.when(when())(work)


FIRST, SECOND, LAST = "la", "bcd", ""


def first_z():
    return lax.axis_index("gz") == 0


def later_z():
    return lax.axis_index("gz") != 0


def sides(z_ev, z_od, y_od, y_ev, *rest):
    refs = dict(zip(NAMES, rest[len(NAMES) :]))

    def assemble_z(odd):
        low, high = (z_ev, z_od) if odd else (z_od, z_ev)

        def body(y, carry):
            for at in range(5):
                frame_of(refs, at)[y + 4, 0:8, :] = fold_halo(at, low, high, y)
            return carry

        lax.fori_loop(0, 16, body, 0, unroll=8)

    def assemble_y(odd):
        low, high = (y_ev, y_od) if odd else (y_od, y_ev)
        for at in range(5):
            n = depth(at)
            for k in range(n):
                lay(refs, at, 4 - n + k, low[3 * at + k])
                lay(refs, at, 20 + k, high[3 * at + k])

    either(is_odd("gz"), assemble_z)
    either(is_odd("gy"), assemble_y)
    sweep("a", refs, [(0, 4), (18, 22)], (8, 16, 24), 4)
    sweep("a", refs, [(4, 18)], (0,), 14)
    sweep("b", refs, [(0, 4), (16, 20)], (8, 16), 4)
    sweep("b", refs, [(4, 16)], (0,), 12)
    sweep("c", refs, [(0, 4), (14, 18)], (8, 16), 4)
    sweep("c", refs, [(4, 14)], (0,), 10)
    sweep("d", refs, [(0, 4), (12, 16)], (8,), 4)
    sweep("d", refs, [(4, 12)], (0,), 8)


def corners(y_od, y_ev, *rest):
    n = len(NAMES)
    refs = dict(zip(NAMES, rest[n : 2 * n]))
    out_red, out_blue, out_mom, sems = rest[2 * n :]

    def send(start, count, sem):
        rows, edge = pl.ds(start, count), refs["edge"]
        pairs = [(edge.at[0, rows], out_red.at[rows]), (edge.at[1, rows], out_blue.at[rows]), (edge.at[2:5, rows], out_mom.at[:, rows])]
        return [pltpu.make_async_copy(src, dst, sems.at[sem, f]) for f, (src, dst) in enumerate(pairs)]

    first = send(4, 8, 0)
    for c in first:
        c.start()

    def assemble(odd):
        low, high = (y_ev, y_od) if odd else (y_od, y_ev)
        for at in range(5):
            d = depth(at)
            for k in range(d):
                frame_of(refs, at)[4 - d + k, 0:8, :] = low[3 * at + k]
                frame_of(refs, at)[20 + k, 0:8, :] = high[3 * at + k]

    either(is_odd("gy"), assemble)
    sweep("a", refs, [(0, 4), (18, 22)], (0,), 4)
    sweep("b", refs, [(0, 4), (16, 20)], (0,), 4)
    sweep("c", refs, [(0, 4), (14, 18)], (0,), 4)
    sweep("d", refs, [(0, 4), (12, 16)], (0,), 4)
    second = send(0, 4, 1) + send(12, 4, 2)
    for c in second:
        c.start()
    for c in first + second:
        c.wait()


def f32(*shape):
    return jax.ShapeDtypeStruct(shape, jnp.float32)


def swap(value, axis, first):
    count = lax.axis_size(axis)
    pairs = []
    for low in range(first, count, 2):
        high = (low + 1) % count
        pairs += [(low, high), (high, low)]
    return lax.ppermute(value, axis, pairs)


def shards(phase, density, velocity):
    phase, density, velocity = [pltpu.with_memory_space_constraint(v, pltpu.HBM) for v in (phase, density, velocity)]
    in_vmem = pl.BlockSpec(memory_space=pltpu.VMEM)
    in_hbm = pl.BlockSpec(memory_space=pltpu.HBM)
    state = [f32(*s) for s in STATE.values()]
    phase, density, velocity, z_ev, z_od, y_od, y_ev = pl.pallas_call(
        pack_own,
        out_shape=(jax.ShapeDtypeStruct((16, 16, 128), jnp.int32), f32(16, 16, 128), f32(3, 16, 16, 128)) + (f32(16, 16, 128),) * 4,
        in_specs=[in_hbm] * 3,
        out_specs=(in_vmem,) * 7,
        scratch_shapes=[pltpu.SemaphoreType.DMA((3,))],
        compiler_params=vmem(8),
    )(phase, density, velocity)
    n = len(NAMES)

    def do_middle(jobs, held, *tokens):
        h, p = len(held), len(tokens)
        made = pl.pallas_call(
            functools.partial(middle, jobs, h, p),
            out_shape=tuple(state) + tuple(jax.ShapeDtypeStruct(t.shape, t.dtype) for t in tokens),
            in_specs=[in_vmem] * (3 + h + p),
            out_specs=(in_vmem,) * (n + p),
            input_output_aliases={3 + i: i + n - h for i in range(h + p)},
            compiler_params=vmem(8),
            cost_estimate=pl.CostEstimate(flops=40_000_000, bytes_accessed=20_000_000, transcendentals=0),
        )(phase, density, velocity, *held, *tokens)
        return made[:n], *made[n:]

    held = []
    if FIRST:
        held, z_ev, z_od = do_middle([(first_z, FIRST)], held, z_ev, z_od)
    z_ev = swap(z_ev, "gz", 0)
    if SECOND:
        held, z_od = do_middle([(first_z, SECOND)], held, z_od)
    z_od = swap(z_od, "gz", 1)
    y_od = swap(y_od, "gy", 1)
    y_ev = swap(y_ev, "gy", 0)
    early = FIRST + SECOND
    jobs = [(later_z, early)] + ([(None, LAST)] if LAST else [])
    held, token = do_middle(jobs, held, jnp.zeros((8, 128), jnp.float32))
    c_od, c_ev = pl.pallas_call(pack_corners, out_shape=(f32(16, 8, 128),) * 2, compiler_params=vmem(4))(z_ev, z_od, token)
    c_od = swap(c_od, "gy", 1)
    c_ev = swap(c_ev, "gy", 0)
    held = pl.pallas_call(
        sides,
        out_shape=tuple(state),
        in_specs=[in_vmem] * (4 + n),
        out_specs=(in_vmem,) * n,
        input_output_aliases={4 + i: i for i in range(n)},
        compiler_params=vmem(8),
        cost_estimate=pl.CostEstimate(flops=10_000_000, bytes_accessed=5_000_000, transcendentals=0),
    )(z_ev, z_od, y_od, y_ev, *held)
    return pl.pallas_call(
        corners,
        out_shape=tuple(state) + (f32(16, 16, 128), f32(16, 16, 128), f32(3, 16, 16, 128)),
        in_specs=[in_vmem] * (2 + n),
        out_specs=(in_vmem,) * n + (in_hbm,) * 3,
        scratch_shapes=[pltpu.SemaphoreType.DMA((3, 3))],
        input_output_aliases={2 + i: i for i in range(n)},
        compiler_params=vmem(8),
    )(c_od, c_ev, *held)[n:]


def solution(mesh):
    placed = (P("gy", "gz", None), P("gy", "gz", None), P(None, "gy", "gz", None))
    return jax.shard_map(
        shards,
        mesh=mesh,
        in_specs=placed,
        out_specs=placed,
        check_vma=False,
    )
```
